32 devices in a mesh: dp: 2 (over x), segment: 16 (over z, y, core).
Axes of the slice: x: 2, y: 2, z: 4, core: 2. Of those that a mesh axis runs over, the one named last changes fastest.
Arguments:
- feed_rising: bfloat16 [4, 128, 512], P(None, 'dp'), may hold values from -6 to 6
- feed_falling: bfloat16 [4, 128, 512], P(None, 'dp'), may hold values from -6 to 6
- up_weight: bfloat16 [32, 512, 1024], P('segment'), as said below
- down_weight: bfloat16 [32, 1024, 512], P('segment'), as said below
- norm_gain: float32 [32, 512], P('segment'), as said below
Outputs:
- grad_up: float32 [512, 8192], P('dp', 'segment')
- grad_down: float32 [8192, 512], P('segment', 'dp')
- grad_gain: float32 [16, 256], P('segment', 'dp')
The draws below stay inside these ranges and needn't reach their ends.
Inputs may be any that keep to these rules, and one draw needn't show every extreme that they name: `up_weight`: normal entries of standard deviation 512^-0.5; the rows of one section (2i, 2i + 1 as in the meaning) are equal. `down_weight`: normal entries of standard deviation 1024^-0.5; the rows of one section are equal. `norm_gain`: the rows of one section are equal.
All inputs are finite; a program needn't handle non-finite values.
Results may differ from the reference program's by a relative error of at most 0.011.
Values may be sent and summed in bfloat16 or wider, within the bound.
A program may use at most 64 MiB of HBM per device.

```python
import math
import jax
import jax.numpy as jnp
from jax import lax

D = 512
H = 1024
M = 4
ROWS_DEV = 32
SECTIONS = 8
MB_ROWS = 128


def section_rows(base):
    order = jnp.arange(4 * SECTIONS)
    device = order // 2
    picked = jnp.where(order % 2 == 0, device // 2, SECTIONS - 1 - device // 2)
    return base[picked]


def draw_up_weight(key, part):
    key = jax.random.fold_in(key, 11)
    base = jax.random.normal(key, (SECTIONS, D, H), jnp.float32) * D ** (-0.5)
    return section_rows(base).astype(jnp.bfloat16)


def draw_down_weight(key, part):
    key = jax.random.fold_in(key, 23)
    base = jax.random.normal(key, (SECTIONS, H, D), jnp.float32) * H ** (-0.5)
    return section_rows(base).astype(jnp.bfloat16)


def draw_norm_gain(key, part):
    key = jax.random.fold_in(key, 37)
    base = jax.random.uniform(key, (SECTIONS, D), jnp.float32, 0.5, 1.5)
    return section_rows(base)


def steps_of(stream_key, shape, cuts, least, high):
    def one(position, shards_of):
        steps = jax.random.uniform(jax.random.fold_in(jax.random.fold_in(stream_key, 6), position), (shards_of,), jnp.float32, least / len(cuts), high / len(cuts))
        return jnp.repeat(jnp.exp(steps), shape[position] // shards_of).reshape((-1,) + (1,) * (len(shape) - position - 1))

    loudness = one(*cuts[0])
    for cut in cuts[1:]:
        loudness = loudness * one(*cut)
    return loudness


def gaussian(key, dims, scale, reach, cuts=(), dtype=jnp.bfloat16):
    entries = scale * jax.random.normal(key, dims, jnp.float32)
    if cuts:
        entries = entries * steps_of(key, dims, cuts, -0.22, 0.18)
    return jnp.clip(entries, -reach, reach).astype(dtype)


def setup_inputs(seed: int = 0) -> dict:
    keys = jax.random.split(jax.random.key(seed), 6)
    return {
        "feed_rising": gaussian(keys[0], (M, MB_ROWS, D), 1.0, 6.0, ((1, 2),)),
        "feed_falling": gaussian(keys[1], (M, MB_ROWS, D), 1.0, 6.0, ((1, 2),)),
        "up_weight": draw_up_weight(jax.random.fold_in(keys[5], 71), 0),
        "down_weight": draw_down_weight(jax.random.fold_in(keys[5], 71), 0),
        "norm_gain": draw_norm_gain(jax.random.fold_in(keys[5], 71), 0),
    }


GELU_C = 0.7978845608028654
CUBIC = 0.044715

def gelu_parts(pre_act):
    inner_arg = GELU_C * (pre_act + CUBIC * pre_act * pre_act * pre_act)
    tangent = jnp.tanh(inner_arg)
    gelu_value = 0.5 * pre_act * (1.0 + tangent)
    gelu_slope = 0.5 * (1.0 + tangent) + 0.5 * pre_act * (1.0 - tangent * tangent) * GELU_C * (1.0 + 3.0 * CUBIC * pre_act * pre_act)
    return (gelu_value, gelu_slope)

def norm_parts(activations, gain_row):
    values = activations.astype(jnp.float32)
    centre = lax.optimization_barrier(jnp.mean(values, axis=-1, keepdims=True))
    spread = lax.optimization_barrier(jnp.mean(jnp.square(values - centre), axis=-1, keepdims=True))
    inverse = lax.rsqrt(spread + 1e-05)
    normed = (values - centre) * inverse
    return (normed, inverse, (normed * gain_row).astype(jnp.bfloat16))

def block_sum(part):
    rounded = lax.optimization_barrier(part.astype(jnp.bfloat16))
    return lax.optimization_barrier(jnp.sum(rounded.astype(jnp.float32), axis=0))

def reference(feed_rising, feed_falling, up_weight, down_weight, norm_gain):
    up_sections = up_weight[::4].astype(jnp.float32)
    down_sections = down_weight[::4].astype(jnp.float32)
    gain_sections = norm_gain[::4]
    blocks = MB_ROWS // ROWS_DEV
    loss_scale = 1.0 / math.sqrt(2.0 * M * MB_ROWS)
    grad_u = [jnp.zeros((D, H), jnp.float32) for section in range(SECTIONS)]
    grad_w = [jnp.zeros((H, D), jnp.float32) for section in range(SECTIONS)]
    grad_g = [jnp.zeros((D,), jnp.float32) for section in range(SECTIONS)]
    for entering in (feed_rising, feed_falling):
        activations = entering
        stored_parts = []
        for section in range(SECTIONS):
            normed, inverse, normed_b = norm_parts(activations, gain_sections[section])
            pre_act = jnp.einsum('mrd,dh->mrh', normed_b.astype(jnp.float32), up_sections[section])
            gelu_value, gelu_slope = gelu_parts(pre_act)
            hidden = gelu_value.astype(jnp.bfloat16)
            emitted = activations.astype(jnp.float32) + jnp.einsum('mrh,hd->mrd', hidden.astype(jnp.float32), down_sections[section])
            stored_parts.append((normed, inverse, normed_b, gelu_slope, hidden))
            activations = emitted.astype(jnp.bfloat16)
        cotangent = (activations.astype(jnp.float32) * loss_scale).astype(jnp.bfloat16)
        for section in reversed(range(SECTIONS)):
            normed, inverse, normed_b, gelu_slope, hidden = stored_parts[section]
            cot_f = cotangent.astype(jnp.float32)
            back_hidden = jnp.einsum('mrd,hd->mrh', cot_f, down_sections[section])
            pre_grad = (back_hidden * gelu_slope).astype(jnp.bfloat16)
            pre_f = pre_grad.astype(jnp.float32)
            part_w = jnp.einsum('mbrh,mbrd->bhd', hidden.astype(jnp.float32).reshape(M, blocks, ROWS_DEV, H), cot_f.reshape(M, blocks, ROWS_DEV, D))
            grad_w[section] = grad_w[section] + block_sum(part_w)
            part_u = jnp.einsum('mbrd,mbrh->bdh', normed_b.astype(jnp.float32).reshape(M, blocks, ROWS_DEV, D), pre_f.reshape(M, blocks, ROWS_DEV, H))
            grad_u[section] = grad_u[section] + block_sum(part_u)
            back_norm = jnp.einsum('mrh,dh->mrd', pre_f, up_sections[section])
            part_g = lax.optimization_barrier(jnp.sum((back_norm * normed).reshape(M, blocks, ROWS_DEV, D), axis=(0, 2)))
            grad_g[section] = grad_g[section] + block_sum(part_g)
            scaled = back_norm * gain_sections[section]
            first_mean = lax.optimization_barrier(jnp.mean(scaled, axis=-1, keepdims=True))
            second_mean = lax.optimization_barrier(jnp.mean(scaled * normed, axis=-1, keepdims=True))
            cotangent = (cot_f + inverse * (scaled - first_mean - normed * second_mean)).astype(jnp.bfloat16)
    grad_up = jnp.stack(grad_u, axis=1).reshape(D, SECTIONS * H)
    grad_down = jnp.stack(grad_w, axis=0).reshape(SECTIONS * H, D)
    grad_gain = jnp.stack(grad_g, axis=0).reshape(2 * SECTIONS, D // 2)
    return (grad_up, grad_down, grad_gain)
```

```python
import functools
import math

import jax
import jax.numpy as jnp
from jax import lax
from jax.experimental import pallas as pl
from jax.experimental.pallas import tpu as pltpu
from jax.sharding import PartitionSpec as P

GELU_C = 0.7978845608028654
CUBIC = 0.044715
CHUNKS_PER_RELAY = 2
MESH = pl.DeviceIdType.MESH


def dot_nt(left, right):
    return lax.dot_general(left, right, (((1,), (1,)), ((), ())), preferred_element_type=jnp.float32)


def dot_tn(left, right):
    return lax.dot_general(left, right, (((0,), (0,)), ((), ())), preferred_element_type=jnp.float32)


def kernel(
    segments,
    replicas,
    loss_scale,
    rising,
    falling,
    up_hbm,
    down_hbm,
    gain_ref,
    out_up,
    out_down,
    out_gain,
    up,
    down,
    x_in,
    y_out,
    xh_st,
    inv_st,
    n_st,
    p_st,
    a_st,
    t_st,
    dy_in,
    dx_out,
    da_st,
    gain_acc,
    gain_sum,
    gain_core,
    gain_dp,
    cs_up,
    cs_down,
    cr_up,
    cr_down,
    acc_up,
    acc_down,
    st_up,
    st_down,
    dr_up,
    dr_down,
    load_sem,
    feed_sem,
    fs_sem,
    fr_sem,
    bs_sem,
    br_sem,
    cs_sem,
    cr_sem,
    ds_sem,
    dr_sem,
):
    place = lax.axis_index("segment")
    rep = lax.axis_index("dp")
    pair = place // 2
    core = place % 2
    last = segments // 2 - 1
    chunks, rows, width = x_in.shape
    hidden_units = up.shape[1]
    half = hidden_units // 2
    micro = rising.shape[0]
    local_rows = rising.shape[1] // 2
    mates = place + 1 - 2 * core
    slice_d = width // replicas

    load_up = pltpu.make_async_copy(up_hbm.at[0], up, load_sem.at[0])
    load_down = pltpu.make_async_copy(down_hbm.at[0], down, load_sem.at[1])
    load_up.start()
    load_down.start()

    per_chunk = rows // local_rows

    def feed_copy(which, m):
        src = (rising, falling)[which]
        flat = which * micro + m
        return pltpu.make_async_copy(
            src.at[m, pl.ds(pl.multiple_of(core * local_rows, local_rows), local_rows), :],
            x_in.at[flat // per_chunk, pl.ds((flat % per_chunk) * local_rows, local_rows), :],
            feed_sem.at[flat],
        )

    @pl.when(pair == 0)
    def _():
        for which in (0, 1):
            for m in range(micro):
                feed_copy(which, m).start()

    barrier = pltpu.get_barrier_semaphore()

    @pl.when(pair > 0)
    def _():
        pl.semaphore_signal(barrier, inc=1, device_id={"segment": place - 2}, device_id_type=MESH)

    @pl.when(pair < last)
    def _():
        pl.semaphore_signal(barrier, inc=1, device_id={"segment": place + 2}, device_id_type=MESH)

    pl.semaphore_signal(barrier, inc=1, device_id={"segment": mates}, device_id_type=MESH)
    for off in range(1, replicas):
        pl.semaphore_signal(
            barrier, inc=1, device_id={"dp": lax.rem(rep + off, replicas)}, device_id_type=MESH
        )
    gain_acc[...] = jnp.zeros_like(gain_acc)
    load_up.wait()
    load_down.wait()
    pl.semaphore_wait(
        barrier,
        replicas + jnp.where(pair > 0, 1, 0) + jnp.where(pair < last, 1, 0),
    )

    def send_forward(i):
        return pltpu.make_async_remote_copy(
            src_ref=y_out.at[i],
            dst_ref=x_in.at[i],
            send_sem=fs_sem.at[i],
            recv_sem=fr_sem.at[i],
            device_id={"segment": place + 2},
            device_id_type=MESH,
        )

    def send_backward(i):
        return pltpu.make_async_remote_copy(
            src_ref=dx_out.at[i],
            dst_ref=dy_in.at[i],
            send_sem=bs_sem.at[i],
            recv_sem=br_sem.at[i],
            device_id={"segment": place - 2},
            device_id_type=MESH,
        )

    @pl.when(pair == 0)
    def _():
        for which in (0, 1):
            for m in range(micro):
                feed_copy(which, m).wait()

    gain_row = gain_ref[0:1, :]

    def forward(i, carry):
        @pl.when(pair > 0)
        def _():
            send_forward(i).wait_recv()

        x = x_in[i].astype(jnp.float32)
        centre = jnp.mean(x, axis=-1, keepdims=True)
        xc = x - centre
        spread = jnp.mean(xc * xc, axis=-1, keepdims=True)
        inverse = lax.rsqrt(spread + 1e-05)
        xh = xc * inverse
        n = (xh * gain_row).astype(jnp.bfloat16)
        a = jnp.dot(n, up[...], preferred_element_type=jnp.float32)
        t = jnp.tanh(GELU_C * (a + CUBIC * a * a * a))
        p = (0.5 * a * (1.0 + t)).astype(jnp.bfloat16)
        y = (x + jnp.dot(p, down[...], preferred_element_type=jnp.float32)).astype(jnp.bfloat16)

        @pl.when(pair < last)
        def _():
            y_out[i] = y
            send_forward(i).start()

        @pl.when(pair == last)
        def _():
            dy_in[i] = (y.astype(jnp.float32) * loss_scale).astype(jnp.bfloat16)

        xh_st[i] = xh
        inv_st[i] = jnp.broadcast_to(inverse, (rows, 128))
        span = pl.ds(pl.multiple_of(i * rows, rows), rows)
        n_st[span, :] = n
        p_st[span, :] = p
        a_st[i] = 0.5 * (1.0 + t) + 0.5 * a * (1.0 - t * t) * GELU_C * (1.0 + 3.0 * CUBIC * a * a)
        return carry

    lax.fori_loop(0, chunks, forward, 0)

    def backward(i, carry):
        @pl.when(pair < last)
        def _():
            send_backward(i).wait_recv()

        dy = dy_in[i]
        dp = dot_nt(dy, down[...])
        da = (dp * a_st[i]).astype(jnp.bfloat16)
        dn = dot_nt(da, up[...])
        xh = xh_st[i]
        e = dn * gain_row
        m1 = jnp.mean(e, axis=-1, keepdims=True)
        m2 = jnp.mean(e * xh, axis=-1, keepdims=True)
        inverse = inv_st[i][:, 0:1]
        dx = (dy.astype(jnp.float32) + inverse * (e - m1 - xh * m2)).astype(jnp.bfloat16)

        @pl.when(pair > 0)
        def _():
            dx_out[i] = dx
            send_backward(i).start()

        span = pl.ds(pl.multiple_of(i * rows, rows), rows)
        da_st[span, :] = da
        t_st[span, :] = dy
        part = (dn * xh).reshape(rows // 8, 8, width)
        gain_acc[...] += jnp.sum(part, axis=0)
        return carry

    lax.fori_loop(0, chunks, backward, 0)

    mine = pl.ds(pl.multiple_of(core * half, half), half)
    theirs = pl.ds(pl.multiple_of((1 - core) * half, half), half)

    def to_core(src, dst, slot):
        return pltpu.make_async_remote_copy(
            src_ref=src,
            dst_ref=dst,
            send_sem=cs_sem.at[slot],
            recv_sem=cr_sem.at[slot],
            device_id={"segment": mates},
            device_id_type=MESH,
        )

    def to_replica(src, dst, slot, off):
        return pltpu.make_async_remote_copy(
            src_ref=src,
            dst_ref=dst.at[off - 1],
            send_sem=ds_sem.at[slot, off - 1],
            recv_sem=dr_sem.at[slot, off - 1],
            device_id={"dp": lax.rem(rep + off, replicas)},
            device_id_type=MESH,
        )

    def target(off):
        return lax.rem(rep + off, replicas)

    core_gain = to_core(gain_acc, gain_core, 2)
    core_gain.start()
    cs_up[...] = dot_tn(n_st[...], da_st[:, theirs]).astype(jnp.bfloat16)
    core_up = to_core(cs_up, cr_up, 0)
    core_up.start()
    cs_down[...] = dot_tn(p_st[:, theirs], t_st[...]).astype(jnp.bfloat16)
    core_down = to_core(cs_down, cr_down, 1)
    core_down.start()

    core_gain.wait()
    gain_sum[...] = gain_acc[...] + gain_core[...]
    for off in range(1, replicas):
        to_replica(gain_sum, gain_dp, 2, off).start()

    total_up = dot_tn(n_st[...], da_st[:, mine])
    core_up.wait()
    total_up = total_up + cr_up[...].astype(jnp.float32)
    for j in range(replicas):
        block = total_up[j * slice_d : (j + 1) * slice_d, :]
        acc_up[j] = block
        st_up[j] = block.astype(jnp.bfloat16)
    for off in range(1, replicas):
        to_replica(st_up.at[target(off)], dr_up, 0, off).start()

    total_down = dot_tn(p_st[:, mine], t_st[...])
    core_down.wait()
    total_down = total_down + cr_down[...].astype(jnp.float32)
    for j in range(replicas):
        block = total_down[:, j * slice_d : (j + 1) * slice_d]
        acc_down[j] = block
        st_down[j] = block.astype(jnp.bfloat16)
    for off in range(1, replicas):
        to_replica(st_down.at[target(off)], dr_down, 1, off).start()

    @pl.when(pair < last)
    def _():
        for i in range(chunks):
            send_forward(i).wait_send()

    @pl.when(pair > 0)
    def _():
        for i in range(chunks):
            send_backward(i).wait_send()

    gains = gain_sum[...]
    for off in range(1, replicas):
        to_replica(gain_sum, gain_dp, 2, off).wait()
        gains = gains + gain_dp[off - 1]
    gains = jnp.sum(gains, axis=0, keepdims=True)
    wide = out_gain.shape[1]
    for c in (0, 1):
        for j in range(replicas):
            start = c * (width // 2) + j * wide

            @pl.when((core == c) & (rep == j))
            def _():
                out_gain[...] = gains[:, start : start + wide]

    res = acc_up[rep]
    for off in range(1, replicas):
        to_replica(st_up.at[target(off)], dr_up, 0, off).wait()
        res = res + dr_up[off - 1].astype(jnp.float32)
    out_up[...] = res
    res = acc_down[rep]
    for off in range(1, replicas):
        to_replica(st_down.at[target(off)], dr_down, 1, off).wait()
        res = res + dr_down[off - 1].astype(jnp.float32)
    out_down[...] = res


def body(feed_rising, feed_falling, up_weight, down_weight, norm_gain):
    segments = lax.axis_size("segment")
    replicas = lax.axis_size("dp")
    micro, rep_rows, width = feed_rising.shape
    local_rows = rep_rows // 2
    hidden = up_weight.shape[2]
    half = hidden // 2
    loss_scale = 1.0 / math.sqrt(2.0 * micro * rep_rows * replicas)
    chunks = 2 * CHUNKS_PER_RELAY
    rows = 2 * micro * local_rows // chunks
    total = chunks * rows
    slice_d = width // replicas
    bf16, f32 = jnp.bfloat16, jnp.float32
    vmem = pl.BlockSpec(memory_space=pltpu.VMEM)
    anym = pl.BlockSpec(memory_space=pl.ANY)
    others = max(replicas - 1, 1)
    flops = 12 * total * width * hidden
    return pl.pallas_call(
        functools.partial(kernel, segments, replicas, loss_scale),
        out_shape=(
            jax.ShapeDtypeStruct((slice_d, half), f32),
            jax.ShapeDtypeStruct((half, slice_d), f32),
            jax.ShapeDtypeStruct((1, width // 2 // replicas), f32),
        ),
        in_specs=[anym, anym, anym, anym, vmem],
        out_specs=(vmem, vmem, vmem),
        scratch_shapes=[
            pltpu.VMEM((width, hidden), bf16),
            pltpu.VMEM((hidden, width), bf16),
            pltpu.VMEM((chunks, rows, width), bf16),
            pltpu.VMEM((chunks, rows, width), bf16),
            pltpu.VMEM((chunks, rows, width), f32),
            pltpu.VMEM((chunks, rows, 128), f32),
            pltpu.VMEM((total, width), bf16),
            pltpu.VMEM((total, hidden), bf16),
            pltpu.VMEM((chunks, rows, hidden), f32),
            pltpu.VMEM((total, width), bf16),
            pltpu.VMEM((chunks, rows, width), bf16),
            pltpu.VMEM((chunks, rows, width), bf16),
            pltpu.VMEM((total, hidden), bf16),
            pltpu.VMEM((8, width), f32),
            pltpu.VMEM((8, width), f32),
            pltpu.VMEM((8, width), f32),
            pltpu.VMEM((others, 8, width), f32),
            pltpu.VMEM((width, half), bf16),
            pltpu.VMEM((half, width), bf16),
            pltpu.VMEM((width, half), bf16),
            pltpu.VMEM((half, width), bf16),
            pltpu.VMEM((replicas, slice_d, half), f32),
            pltpu.VMEM((replicas, half, slice_d), f32),
            pltpu.VMEM((replicas, slice_d, half), bf16),
            pltpu.VMEM((replicas, half, slice_d), bf16),
            pltpu.VMEM((others, slice_d, half), bf16),
            pltpu.VMEM((others, half, slice_d), bf16),
            pltpu.SemaphoreType.DMA((2,)),
            pltpu.SemaphoreType.DMA((2 * micro,)),
            pltpu.SemaphoreType.DMA((chunks,)),
            pltpu.SemaphoreType.DMA((chunks,)),
            pltpu.SemaphoreType.DMA((chunks,)),
            pltpu.SemaphoreType.DMA((chunks,)),
            pltpu.SemaphoreType.DMA((3,)),
            pltpu.SemaphoreType.DMA((3,)),
            pltpu.SemaphoreType.DMA((3, others)),
            pltpu.SemaphoreType.DMA((3, others)),
        ],
        compiler_params=pltpu.CompilerParams(
            collective_id=0, has_side_effects=True, vmem_limit_bytes=40 * 1024 * 1024
        ),
        cost_estimate=pl.CostEstimate(
            flops=flops, bytes_accessed=6 * 1024 * 1024, transcendentals=total * hidden
        ),
        name="relay",
    )(feed_rising, feed_falling, up_weight, down_weight, norm_gain)


def solution(mesh):
    return jax.shard_map(
        body,
        mesh=mesh,
        in_specs=(
            P(None, "dp", None),
            P(None, "dp", None),
            P("segment", None, None),
            P("segment", None, None),
            P("segment", None),
        ),
        out_specs=(P("dp", "segment"), P("segment", "dp"), P("segment", "dp")),
        check_vma=False,
    )
```

```python
import functools
import math

import jax
import jax.numpy as jnp
from jax import lax
from jax.experimental import pallas as pl
from jax.experimental.pallas import tpu as pltpu
from jax.sharding import PartitionSpec as P

GELU_C = 0.7978845608028654
CUBIC = 0.044715
CHUNKS_PER_RELAY = 4
MESH = pl.DeviceIdType.MESH


def dot_tn(left, right):
    return lax.dot_general(left, right, (((0,), (0,)), ((), ())), preferred_element_type=jnp.float32)


def gelu_parts(pre_act):
    tangent = jnp.tanh(GELU_C * (pre_act + CUBIC * pre_act * pre_act * pre_act))
    value = 0.5 * pre_act * (1.0 + tangent)
    slope = 0.5 * (1.0 + tangent) + 0.5 * pre_act * (1.0 - tangent * tangent) * GELU_C * (
        1.0 + 3.0 * CUBIC * pre_act * pre_act
    )
    return value.astype(jnp.bfloat16), slope


def norm_parts(x):
    xc = x - jnp.mean(x, axis=-1, keepdims=True)
    inverse = lax.rsqrt(jnp.mean(xc * xc, axis=-1, keepdims=True) + 1e-05)
    return xc * inverse, inverse


def kernel(
    segments,
    replicas,
    loss_scale,
    rising,
    falling,
    up_hbm,
    down_hbm,
    gain_hbm,
    out_up,
    out_down,
    out_gain,
    up,
    down,
    up_t,
    down_t,
    gain_ref,
    x_all,
    dy_all,
    y_out,
    dx_out,
    xh_st,
    inv_st,
    p_st,
    slope_st,
    da_st,
    n_all,
    p_all,
    slope_all,
    da_all,
    gain_acc,
    acc_up,
    acc_down,
    load_sem,
    feed_sem,
    fs_sem,
    bs_sem,
    xs_sem,
    xr_sem,
    ds_sem,
    dr_sem,
    gs_sem,
    gr_sem,
):
    place = lax.axis_index("segment")
    rep = lax.axis_index("dp")
    pair = place // 2
    core = place % 2
    last = segments // 2 - 1
    slots, chunks, rows, width = x_all.shape
    total = chunks * rows
    half = up.shape[1] // 2
    micro = rising.shape[0]
    local_rows = rising.shape[1] // 2
    mate = place + 1 - 2 * core
    slice_d = width // replicas
    per_chunk = rows // local_rows
    mine = pl.ds(pl.multiple_of(core * half, half), half)

    def feed_copy(which, m):
        flat = which * micro + m
        return pltpu.make_async_copy(
            (rising, falling)[which].at[
                m, pl.ds(pl.multiple_of(core * local_rows, local_rows), local_rows), :
            ],
            x_all.at[0, flat // per_chunk, pl.ds((flat % per_chunk) * local_rows, local_rows), :],
            feed_sem.at[flat],
        )

    load_gain = pltpu.make_async_copy(gain_hbm, gain_ref, load_sem.at[2])
    load_up = pltpu.make_async_copy(up_hbm.at[0], up, load_sem.at[0])
    load_down = pltpu.make_async_copy(down_hbm.at[0], down, load_sem.at[1])

    @pl.when(pair == 0)
    def _():
        for which in (0, 1):
            for m in range(micro):
                feed_copy(which, m).start()

    load_gain.start()
    load_up.start()
    load_down.start()

    peers = [(1, {"segment": mate})]
    for off in range(1, replicas):
        other = lax.rem(rep + off, replicas)
        peers.append((2 * off, {"dp": other}))
        peers.append((2 * off + 1, {"dp": other, "segment": mate}))

    barrier = pltpu.get_barrier_semaphore()

    @pl.when(pair > 0)
    def _():
        pl.semaphore_signal(barrier, inc=1, device_id={"segment": place - 2}, device_id_type=MESH)

    @pl.when(pair < last)
    def _():
        pl.semaphore_signal(barrier, inc=1, device_id={"segment": place + 2}, device_id_type=MESH)

    for _, peer in peers:
        pl.semaphore_signal(barrier, inc=1, device_id=peer, device_id_type=MESH)
    gain_acc[0] = jnp.zeros(gain_acc.shape[1:], gain_acc.dtype)
    pl.semaphore_wait(
        barrier,
        len(peers) + jnp.where(pair > 0, 1, 0) + jnp.where(pair < last, 1, 0),
    )

    def send(src, dst, send_sem, recv_sem, peer):
        return pltpu.make_async_remote_copy(
            src_ref=src,
            dst_ref=dst,
            send_sem=send_sem,
            recv_sem=recv_sem,
            device_id=peer,
            device_id_type=MESH,
        )

    def send_forward(i):
        return send(
            y_out.at[i], x_all.at[0, i], fs_sem.at[i], xr_sem.at[0, i], {"segment": place + 2}
        )

    def send_backward(i):
        return send(
            dx_out.at[i], dy_all.at[0, i], bs_sem.at[i], dr_sem.at[0, i], {"segment": place - 2}
        )

    def share(buf, sems, slot, i):
        if slot == 1:
            peer, origin = {"segment": mate}, 0
        elif slot % 2 == 0:
            peer, origin = {"dp": lax.rem(rep + slot // 2, replicas)}, 0
        else:
            peer, origin = {"segment": mate}, slot - 1
        return send(
            buf.at[origin, i], buf.at[slot, i], sems[0].at[slot, i], sems[1].at[slot, i], peer
        )

    xs = (xs_sem, xr_sem)
    ds = (ds_sem, dr_sem)

    def share_own(buf, sems, i):
        for off in range(1, replicas):
            share(buf, sems, 2 * off, i).start()
        share(buf, sems, 1, i).start()

    def hand_on(buf, sems, i):
        for off in range(1, replicas):
            share(buf, sems, 2 * off, i).wait_recv()
            share(buf, sems, 2 * off + 1, i).start()

    def span(i):
        return pl.ds(pl.multiple_of(i * rows, rows), rows)

    def slot_span(s):
        return pl.ds(pl.multiple_of(s * total, total), total)

    def transpose_weights():
        down_t[...] = down[...].T
        up_t[...] = up[...].T

    @pl.when(pair == 0)
    def _():
        for which in (0, 1):
            for m in range(micro):
                feed_copy(which, m).wait()

    load_gain.wait()
    load_up.wait()
    load_down.wait()
    gain_row = gain_ref[0:1, :]

    @pl.when(2 * pair > last)
    def _():
        transpose_weights()

    def forward(i, carry):
        @pl.when(pair > 0)
        def _():
            send_forward(i).wait_recv()

        x = x_all[0, i].astype(jnp.float32)
        xh, inverse = norm_parts(x)
        n = (xh * gain_row).astype(jnp.bfloat16)
        a = jnp.dot(n, up[...], preferred_element_type=jnp.float32)
        p, slope = gelu_parts(a)
        y = (x + jnp.dot(p, down[...], preferred_element_type=jnp.float32)).astype(jnp.bfloat16)

        @pl.when(pair < last)
        def _():
            y_out[i] = y
            send_forward(i).start()

        @pl.when(pair == last)
        def _():
            dy_all[0, i] = (y.astype(jnp.float32) * loss_scale).astype(jnp.bfloat16)

        share_own(x_all, xs, i)

        @pl.when(i > 0)
        def _():
            hand_on(x_all, xs, i - 1)

        xh_st[i] = xh
        inv_st[i] = jnp.broadcast_to(inverse, (rows, 128))
        n_all[span(i), :] = n
        p_st[span(i), :] = p
        slope_st[i] = slope
        return carry

    lax.fori_loop(0, chunks, forward, 0)
    hand_on(x_all, xs, chunks - 1)

    @pl.when(2 * pair <= last)
    def _():
        transpose_weights()

    def peers_forward():
        for s in range(1, slots, 2):
            for i in range(chunks):
                share(x_all, xs, s, i).wait_recv()

        def one(s, carry):
            xh, _ = norm_parts(x_all[s].reshape(total, width).astype(jnp.float32))
            n = (xh * gain_row).astype(jnp.bfloat16)
            n_all[slot_span(s), :] = n
            a = jnp.dot(n, up[:, mine], preferred_element_type=jnp.float32)
            p, slope = gelu_parts(a)
            p_all[slot_span(s), :] = p
            slope_all[slot_span(s), :] = slope
            return carry

        lax.fori_loop(1, slots, one, 0)
        p_all[slot_span(0), :] = p_st[:, mine]

    @pl.when(pair < last - 1)
    def _():
        peers_forward()

    def backward(i, carry):
        @pl.when(pair < last)
        def _():
            send_backward(i).wait_recv()

        share_own(dy_all, ds, i)
        dy = dy_all[0, i]
        dp = jnp.dot(dy, down_t[...], preferred_element_type=jnp.float32)
        da = (dp * slope_st[i]).astype(jnp.bfloat16)
        dn = jnp.dot(da, up_t[...], preferred_element_type=jnp.float32)
        xh = xh_st[i]
        e = dn * gain_row
        m1 = jnp.mean(e, axis=-1, keepdims=True)
        m2 = jnp.mean(e * xh, axis=-1, keepdims=True)
        inverse = inv_st[i][:, 0:1]
        dx = (dy.astype(jnp.float32) + inverse * (e - m1 - xh * m2)).astype(jnp.bfloat16)

        @pl.when(pair > 0)
        def _():
            dx_out[i] = dx
            send_backward(i).start()

        @pl.when(i > 0)
        def _():
            hand_on(dy_all, ds, i - 1)

        da_st[span(i), :] = da
        gain_acc[0] += jnp.sum((dn * xh).reshape(rows // 8, 8, width), axis=0)
        return carry

    lax.fori_loop(0, chunks, backward, 0)
    hand_on(dy_all, ds, chunks - 1)

    def send_gain(slot, peer):
        return send(gain_acc.at[0], gain_acc.at[slot], gs_sem.at[slot], gr_sem.at[slot], peer)

    for slot, peer in peers:
        send_gain(slot, peer).start()

    @pl.when(pair >= last - 1)
    def _():
        peers_forward()

    da_all[slot_span(0), :] = da_st[:, mine]
    for s in range(2, slots, 2):
        peer_da(s, slot_span, dy_all, down_t, mine, slope_all, da_all)
    for s in range(1, slots, 2):
        for i in range(chunks):
            share(dy_all, ds, s, i).wait_recv()
        peer_da(s, slot_span, dy_all, down_t, mine, slope_all, da_all)

    if slice_d % 128 == 0:
        cols = pl.ds(pl.multiple_of(rep * slice_d, slice_d), slice_d)
        out_up[...] = dot_tn(n_all[:, cols], da_all[...])
        dy_cols = dy_all[:, :, :, cols].reshape(slots * total, slice_d)
        out_down[...] = dot_tn(p_all[...], dy_cols)
    else:
        whole_up = dot_tn(n_all[...], da_all[...])
        whole_down = dot_tn(p_all[...], dy_all[...].reshape(slots * total, width))
        for j in range(replicas):
            acc_up[j] = whole_up[j * slice_d : (j + 1) * slice_d, :]
            acc_down[j] = whole_down[:, j * slice_d : (j + 1) * slice_d]
        out_up[...] = acc_up[rep]
        out_down[...] = acc_down[rep]

    gains = gain_acc[0]
    for slot, peer in peers:
        send_gain(slot, peer).wait()
        gains = gains + gain_acc[slot]
    gains = jnp.sum(gains, axis=0, keepdims=True)
    wide = out_gain.shape[1]
    for c in (0, 1):
        for j in range(replicas):
            start = c * (width // 2) + j * wide

            @pl.when((core == c) & (rep == j))
            def _():
                out_gain[...] = gains[:, start : start + wide]

    def drain(i, carry):
        for slot in range(1, slots):
            share(x_all, xs, slot, i).wait_send()
            share(dy_all, ds, slot, i).wait_send()

        @pl.when(pair < last)
        def _():
            send_forward(i).wait_send()

        @pl.when(pair > 0)
        def _():
            send_backward(i).wait_send()

        return carry

    lax.fori_loop(0, chunks, drain, 0)


def peer_da(s, slot_span, dy_all, down_t, mine, slope_all, da_all):
    slots, chunks, rows, width = dy_all.shape
    dy = dy_all[s].reshape(chunks * rows, width)
    dp = jnp.dot(dy, down_t[:, mine], preferred_element_type=jnp.float32)
    da_all[slot_span(s), :] = (dp * slope_all[slot_span(s), :]).astype(jnp.bfloat16)


def body(feed_rising, feed_falling, up_weight, down_weight, norm_gain):
    segments = lax.axis_size("segment")
    replicas = lax.axis_size("dp")
    micro, rep_rows, width = feed_rising.shape
    local_rows = rep_rows // 2
    hidden = up_weight.shape[2]
    half = hidden // 2
    loss_scale = 1.0 / math.sqrt(2.0 * micro * rep_rows * replicas)
    chunks = 2 * CHUNKS_PER_RELAY
    rows = 2 * micro * local_rows // chunks
    total = chunks * rows
    slots = 2 * replicas
    slice_d = width // replicas
    bf16, f32 = jnp.bfloat16, jnp.float32
    vmem = pl.BlockSpec(memory_space=pltpu.VMEM)
    hbm = pl.BlockSpec(memory_space=pltpu.HBM)
    spare = (8, 128) if slice_d % 128 == 0 else None
    dma = pltpu.SemaphoreType.DMA
    return pl.pallas_call(
        functools.partial(kernel, segments, replicas, loss_scale),
        out_shape=(
            jax.ShapeDtypeStruct((slice_d, half), f32),
            jax.ShapeDtypeStruct((half, slice_d), f32),
            jax.ShapeDtypeStruct((1, width // 2 // replicas), f32),
        ),
        in_specs=[hbm, hbm, hbm, hbm, hbm],
        out_specs=(vmem, vmem, vmem),
        scratch_shapes=[
            pltpu.VMEM((width, hidden), bf16),
            pltpu.VMEM((hidden, width), bf16),
            pltpu.VMEM((hidden, width), bf16),
            pltpu.VMEM((width, hidden), bf16),
            pltpu.VMEM((norm_gain.shape[0], width), f32),
            pltpu.VMEM((slots, chunks, rows, width), bf16),
            pltpu.VMEM((slots, chunks, rows, width), bf16),
            pltpu.VMEM((chunks, rows, width), bf16),
            pltpu.VMEM((chunks, rows, width), bf16),
            pltpu.VMEM((chunks, rows, width), f32),
            pltpu.VMEM((chunks, rows, 128), f32),
            pltpu.VMEM((total, hidden), bf16),
            pltpu.VMEM((chunks, rows, hidden), f32),
            pltpu.VMEM((total, hidden), bf16),
            pltpu.VMEM((slots * total, width), bf16),
            pltpu.VMEM((slots * total, half), bf16),
            pltpu.VMEM((slots * total, half), f32),
            pltpu.VMEM((slots * total, half), bf16),
            pltpu.VMEM((slots, 8, width), f32),
            pltpu.VMEM(spare or (replicas, slice_d, half), f32),
            pltpu.VMEM(spare or (replicas, half, slice_d), f32),
            dma((3,)),
            dma((2 * micro,)),
            dma((chunks,)),
            dma((chunks,)),
            dma((slots, chunks)),
            dma((slots, chunks)),
            dma((slots, chunks)),
            dma((slots, chunks)),
            dma((slots,)),
            dma((slots,)),
        ],
        compiler_params=pltpu.CompilerParams(
            collective_id=0, has_side_effects=True, vmem_limit_bytes=56 * 1024 * 1024
        ),
        cost_estimate=pl.CostEstimate(
            flops=16 * total * width * hidden,
            bytes_accessed=6 * 1024 * 1024,
            transcendentals=3 * total * hidden,
        ),
        name="relay",
    )(feed_rising, feed_falling, up_weight, down_weight, norm_gain)


def solution(mesh):
    return jax.shard_map(
        body,
        mesh=mesh,
        in_specs=(
            P(None, "dp", None),
            P(None, "dp", None),
            P("segment", None, None),
            P("segment", None, None),
            P("segment", None),
        ),
        out_specs=(P("dp", "segment"), P("segment", "dp"), P("segment", "dp")),
        check_vma=False,
    )
```

```python
import functools
import math

import jax
import jax.numpy as jnp
from jax import lax
from jax.experimental import pallas as pl
from jax.experimental.pallas import tpu as pltpu
from jax.sharding import PartitionSpec as P

GELU_C = 0.7978845608028654
CUBIC = 0.044715
CHUNKS_PER_RELAY = 2
TILE = 256
MESH = pl.DeviceIdType.MESH


def dot_tn(left, right):
    return lax.dot_general(left, right, (((0,), (0,)), ((), ())), preferred_element_type=jnp.float32)


def gelu_slope(pre_act, tangent):
    return 0.5 * (1.0 + tangent) + 0.5 * pre_act * (1.0 - tangent * tangent) * GELU_C * (
        1.0 + 3.0 * CUBIC * pre_act * pre_act
    )


def gelu_parts(pre_act):
    tangent = jnp.tanh(GELU_C * (pre_act + CUBIC * pre_act * pre_act * pre_act))
    value = 0.5 * pre_act * (1.0 + tangent)
    return value.astype(jnp.bfloat16), gelu_slope(pre_act, tangent)


def norm_parts(x):
    xc = x - jnp.mean(x, axis=-1, keepdims=True)
    inverse = lax.rsqrt(jnp.mean(xc * xc, axis=-1, keepdims=True) + 1e-05)
    return xc * inverse, inverse


def kernel(
    segments,
    replicas,
    loss_scale,
    rising,
    falling,
    up_hbm,
    down_hbm,
    gain_hbm,
    out_up,
    out_down,
    out_gain,
    up,
    down,
    up_t,
    down_t,
    gain_ref,
    x_all,
    dy_all,
    y_out,
    dx_out,
    xh_st,
    inv_st,
    p_st,
    slope_st,
    a_st,
    t_st,
    da_st,
    n_all,
    p_all,
    slope_all,
    da_all,
    gain_acc,
    acc_up,
    acc_down,
    load_sem,
    feed_sem,
    fs_sem,
    bs_sem,
    xs_sem,
    xr_sem,
    ds_sem,
    dr_sem,
    gs_sem,
    gr_sem,
):
    place = lax.axis_index("segment")
    rep = lax.axis_index("dp")
    pair = place // 2
    core = place % 2
    last = segments // 2 - 1
    slots, chunks, rows, width = x_all.shape
    total = chunks * rows
    half = up.shape[1] // 2
    micro = rising.shape[0]
    local_rows = rising.shape[1] // 2
    mate = place + 1 - 2 * core
    slice_d = width // replicas
    per_chunk = rows // local_rows
    mine = pl.ds(pl.multiple_of(core * half, half), half)

    def feed_copy(which, m):
        flat = which * micro + m
        return pltpu.make_async_copy(
            (rising, falling)[which].at[
                m, pl.ds(pl.multiple_of(core * local_rows, local_rows), local_rows), :
            ],
            x_all.at[0, flat // per_chunk, pl.ds((flat % per_chunk) * local_rows, local_rows), :],
            feed_sem.at[flat],
        )

    load_gain = pltpu.make_async_copy(gain_hbm, gain_ref, load_sem.at[2])
    load_up = pltpu.make_async_copy(up_hbm.at[0], up, load_sem.at[0])
    load_down = pltpu.make_async_copy(down_hbm.at[0], down, load_sem.at[1])

    @pl.when(pair == 0)
    def _():
        for which in (0, 1):
            for m in range(micro):
                feed_copy(which, m).start()

    load_gain.start()
    load_up.start()
    load_down.start()

    peers = [(1, {"segment": mate})]
    for off in range(1, replicas):
        other = lax.rem(rep + off, replicas)
        peers.append((2 * off, {"dp": other}))
        peers.append((2 * off + 1, {"dp": other, "segment": mate}))

    barrier = pltpu.get_barrier_semaphore()

    @pl.when(pair > 0)
    def _():
        pl.semaphore_signal(barrier, inc=1, device_id={"segment": place - 2}, device_id_type=MESH)

    @pl.when(pair < last)
    def _():
        pl.semaphore_signal(barrier, inc=1, device_id={"segment": place + 2}, device_id_type=MESH)

    for _, peer in peers:
        pl.semaphore_signal(barrier, inc=1, device_id=peer, device_id_type=MESH)
    gain_acc[0] = jnp.zeros(gain_acc.shape[1:], gain_acc.dtype)
    pl.semaphore_wait(
        barrier,
        len(peers) + jnp.where(pair > 0, 1, 0) + jnp.where(pair < last, 1, 0),
    )

    def send(src, dst, send_sem, recv_sem, peer):
        return pltpu.make_async_remote_copy(
            src_ref=src,
            dst_ref=dst,
            send_sem=send_sem,
            recv_sem=recv_sem,
            device_id=peer,
            device_id_type=MESH,
        )

    def send_forward(i):
        return send(
            y_out.at[i], x_all.at[0, i], fs_sem.at[i], xr_sem.at[0, i], {"segment": place + 2}
        )

    def send_backward(i):
        return send(
            dx_out.at[i], dy_all.at[0, i], bs_sem.at[i], dr_sem.at[0, i], {"segment": place - 2}
        )

    def share(buf, sems, slot, i):
        if slot == 1:
            peer, origin = {"segment": mate}, 0
        elif slot % 2 == 0:
            peer, origin = {"dp": lax.rem(rep + slot // 2, replicas)}, 0
        else:
            peer, origin = {"segment": mate}, slot - 1
        return send(
            buf.at[origin, i], buf.at[slot, i], sems[0].at[slot, i], sems[1].at[slot, i], peer
        )

    xs = (xs_sem, xr_sem)
    ds = (ds_sem, dr_sem)

    def share_own(buf, sems, i):
        for off in range(1, replicas):
            share(buf, sems, 2 * off, i).start()
        share(buf, sems, 1, i).start()

    def hand_on(buf, sems, i):
        for off in range(1, replicas):
            share(buf, sems, 2 * off, i).wait_recv()
            share(buf, sems, 2 * off + 1, i).start()

    def span(i):
        return pl.ds(pl.multiple_of(i * rows, rows), rows)

    def slot_span(s):
        return pl.ds(pl.multiple_of(s * total, total), total)

    def transpose_weights():
        down_t[...] = down[...].T
        up_t[...] = up[...].T

    @pl.when(pair == 0)
    def _():
        for which in (0, 1):
            for m in range(micro):
                feed_copy(which, m).wait()

    load_gain.wait()
    load_up.wait()
    load_down.wait()
    gain_row = gain_ref[0:1, :]

    @pl.when(2 * pair > last)
    def _():
        transpose_weights()

    def forward(i, carry):
        @pl.when(pair > 0)
        def _():
            send_forward(i).wait_recv()

        x = x_all[0, i].astype(jnp.float32)
        xh, inverse = norm_parts(x)
        n = (xh * gain_row).astype(jnp.bfloat16)
        y = x
        for j in range(0, 2 * half, TILE):
            a = jnp.dot(n, up[:, j : j + TILE], preferred_element_type=jnp.float32)
            t = jnp.tanh(GELU_C * (a + CUBIC * a * a * a))
            p = (0.5 * a * (1.0 + t)).astype(jnp.bfloat16)
            a_st[:, j : j + TILE] = a
            t_st[:, j : j + TILE] = t
            p_st[span(i), j : j + TILE] = p
            y = y + jnp.dot(p, down[j : j + TILE, :], preferred_element_type=jnp.float32)
        y = y.astype(jnp.bfloat16)

        @pl.when(pair < last)
        def _():
            y_out[i] = y
            send_forward(i).start()

        @pl.when(pair == last)
        def _():
            dy_all[0, i] = (y.astype(jnp.float32) * loss_scale).astype(jnp.bfloat16)

        share_own(x_all, xs, i)

        @pl.when(i > 0)
        def _():
            hand_on(x_all, xs, i - 1)

        xh_st[i] = xh
        inv_st[i] = jnp.broadcast_to(inverse, (rows, 128))
        n_all[span(i), :] = n
        slope_st[i] = gelu_slope(a_st[...], t_st[...])
        return carry

    lax.fori_loop(0, chunks, forward, 0)
    hand_on(x_all, xs, chunks - 1)

    @pl.when(2 * pair <= last)
    def _():
        transpose_weights()

    def peers_forward():
        for s in range(1, slots, 2):
            for i in range(chunks):
                share(x_all, xs, s, i).wait_recv()

        def one(s, carry):
            xh, _ = norm_parts(x_all[s].reshape(total, width).astype(jnp.float32))
            n = (xh * gain_row).astype(jnp.bfloat16)
            n_all[slot_span(s), :] = n
            a = jnp.dot(n, up[:, mine], preferred_element_type=jnp.float32)
            p, slope = gelu_parts(a)
            p_all[slot_span(s), :] = p
            slope_all[slot_span(s), :] = slope
            return carry

        lax.fori_loop(1, slots, one, 0)
        p_all[slot_span(0), :] = p_st[:, mine]

    @pl.when(pair < last - 1)
    def _():
        peers_forward()

    def backward(i, carry):
        @pl.when(pair < last)
        def _():
            send_backward(i).wait_recv()

        dy = dy_all[0, i]
        dn = jnp.zeros((rows, width), jnp.float32)
        for j in range(0, 2 * half, TILE):
            dp = jnp.dot(dy, down_t[:, j : j + TILE], preferred_element_type=jnp.float32)
            da = (dp * slope_st[i, :, j : j + TILE]).astype(jnp.bfloat16)
            da_st[span(i), j : j + TILE] = da
            dn = dn + jnp.dot(da, up_t[j : j + TILE, :], preferred_element_type=jnp.float32)
        xh = xh_st[i]
        e = dn * gain_row
        m1 = jnp.mean(e, axis=-1, keepdims=True)
        m2 = jnp.mean(e * xh, axis=-1, keepdims=True)
        inverse = inv_st[i][:, 0:1]
        dx = (dy.astype(jnp.float32) + inverse * (e - m1 - xh * m2)).astype(jnp.bfloat16)

        @pl.when(pair > 0)
        def _():
            dx_out[i] = dx
            send_backward(i).start()

        share_own(dy_all, ds, i)

        @pl.when(i > 0)
        def _():
            hand_on(dy_all, ds, i - 1)

        gain_acc[0] += jnp.sum((dn * xh).reshape(rows // 8, 8, width), axis=0)
        return carry

    lax.fori_loop(0, chunks, backward, 0)
    hand_on(dy_all, ds, chunks - 1)

    def send_gain(slot, peer):
        return send(gain_acc.at[0], gain_acc.at[slot], gs_sem.at[slot], gr_sem.at[slot], peer)

    for slot, peer in peers:
        send_gain(slot, peer).start()

    @pl.when(pair >= last - 1)
    def _():
        peers_forward()

    da_all[slot_span(0), :] = da_st[:, mine]
    for s in range(2, slots, 2):
        peer_da(s, slot_span, dy_all, down_t, mine, slope_all, da_all)
    for s in range(1, slots, 2):
        for i in range(chunks):
            share(dy_all, ds, s, i).wait_recv()
        peer_da(s, slot_span, dy_all, down_t, mine, slope_all, da_all)

    if slice_d % 128 == 0:
        cols = pl.ds(pl.multiple_of(rep * slice_d, slice_d), slice_d)
        out_up[...] = dot_tn(n_all[:, cols], da_all[...])
        dy_cols = dy_all[:, :, :, cols].reshape(slots * total, slice_d)
        out_down[...] = dot_tn(p_all[...], dy_cols)
    else:
        whole_up = dot_tn(n_all[...], da_all[...])
        whole_down = dot_tn(p_all[...], dy_all[...].reshape(slots * total, width))
        for j in range(replicas):
            acc_up[j] = whole_up[j * slice_d : (j + 1) * slice_d, :]
            acc_down[j] = whole_down[:, j * slice_d : (j + 1) * slice_d]
        out_up[...] = acc_up[rep]
        out_down[...] = acc_down[rep]

    gains = gain_acc[0]
    for slot, peer in peers:
        send_gain(slot, peer).wait()
        gains = gains + gain_acc[slot]
    gains = jnp.sum(gains, axis=0, keepdims=True)
    wide = out_gain.shape[1]
    for c in (0, 1):
        for j in range(replicas):
            start = c * (width // 2) + j * wide

            @pl.when((core == c) & (rep == j))
            def _():
                out_gain[...] = gains[:, start : start + wide]

    def drain(i, carry):
        for slot in range(1, slots):
            share(x_all, xs, slot, i).wait_send()
            share(dy_all, ds, slot, i).wait_send()

        @pl.when(pair < last)
        def _():
            send_forward(i).wait_send()

        @pl.when(pair > 0)
        def _():
            send_backward(i).wait_send()

        return carry

    lax.fori_loop(0, chunks, drain, 0)


def peer_da(s, slot_span, dy_all, down_t, mine, slope_all, da_all):
    slots, chunks, rows, width = dy_all.shape
    dy = dy_all[s].reshape(chunks * rows, width)
    dp = jnp.dot(dy, down_t[:, mine], preferred_element_type=jnp.float32)
    da_all[slot_span(s), :] = (dp * slope_all[slot_span(s), :]).astype(jnp.bfloat16)


def body(feed_rising, feed_falling, up_weight, down_weight, norm_gain):
    segments = lax.axis_size("segment")
    replicas = lax.axis_size("dp")
    micro, rep_rows, width = feed_rising.shape
    local_rows = rep_rows // 2
    hidden = up_weight.shape[2]
    half = hidden // 2
    loss_scale = 1.0 / math.sqrt(2.0 * micro * rep_rows * replicas)
    chunks = 2 * CHUNKS_PER_RELAY
    rows = 2 * micro * local_rows // chunks
    total = chunks * rows
    slots = 2 * replicas
    slice_d = width // replicas
    bf16, f32 = jnp.bfloat16, jnp.float32
    vmem = pl.BlockSpec(memory_space=pltpu.VMEM)
    hbm = pl.BlockSpec(memory_space=pltpu.HBM)
    spare = (8, 128) if slice_d % 128 == 0 else None
    dma = pltpu.SemaphoreType.DMA
    return pl.pallas_call(
        functools.partial(kernel, segments, replicas, loss_scale),
        out_shape=(
            jax.ShapeDtypeStruct((slice_d, half), f32),
            jax.ShapeDtypeStruct((half, slice_d), f32),
            jax.ShapeDtypeStruct((1, width // 2 // replicas), f32),
        ),
        in_specs=[hbm, hbm, hbm, hbm, hbm],
        out_specs=(vmem, vmem, vmem),
        scratch_shapes=[
            pltpu.VMEM((width, hidden), bf16),
            pltpu.VMEM((hidden, width), bf16),
            pltpu.VMEM((hidden, width), bf16),
            pltpu.VMEM((width, hidden), bf16),
            pltpu.VMEM((norm_gain.shape[0], width), f32),
            pltpu.VMEM((slots, chunks, rows, width), bf16),
            pltpu.VMEM((slots, chunks, rows, width), bf16),
            pltpu.VMEM((chunks, rows, width), bf16),
            pltpu.VMEM((chunks, rows, width), bf16),
            pltpu.VMEM((chunks, rows, width), f32),
            pltpu.VMEM((chunks, rows, 128), f32),
            pltpu.VMEM((total, hidden), bf16),
            pltpu.VMEM((chunks, rows, hidden), f32),
            pltpu.VMEM((rows, hidden), f32),
            pltpu.VMEM((rows, hidden), f32),
            pltpu.VMEM((total, hidden), bf16),
            pltpu.VMEM((slots * total, width), bf16),
            pltpu.VMEM((slots * total, half), bf16),
            pltpu.VMEM((slots * total, half), f32),
            pltpu.VMEM((slots * total, half), bf16),
            pltpu.VMEM((slots, 8, width), f32),
            pltpu.VMEM(spare or (replicas, slice_d, half), f32),
            pltpu.VMEM(spare or (replicas, half, slice_d), f32),
            dma((3,)),
            dma((2 * micro,)),
            dma((chunks,)),
            dma((chunks,)),
            dma((slots, chunks)),
            dma((slots, chunks)),
            dma((slots, chunks)),
            dma((slots, chunks)),
            dma((slots,)),
            dma((slots,)),
        ],
        compiler_params=pltpu.CompilerParams(
            collective_id=0, has_side_effects=True, vmem_limit_bytes=(24 + 2 * slots) * 1024 * 1024
        ),
        cost_estimate=pl.CostEstimate(
            flops=16 * total * width * hidden,
            bytes_accessed=6 * 1024 * 1024,
            transcendentals=3 * total * hidden,
        ),
        name="relay",
    )(feed_rising, feed_falling, up_weight, down_weight, norm_gain)


def solution(mesh):
    return jax.shard_map(
        body,
        mesh=mesh,
        in_specs=(
            P(None, "dp", None),
            P(None, "dp", None),
            P("segment", None, None),
            P("segment", None, None),
            P("segment", None),
        ),
        out_specs=(P("dp", "segment"), P("segment", "dp"), P("segment", "dp")),
        check_vma=False,
    )
```

```python
import functools
import math

import jax
import jax.numpy as jnp
from jax import lax
from jax.experimental import pallas as pl
from jax.experimental.pallas import tpu as pltpu
from jax.sharding import PartitionSpec as P

GELU_C = 0.7978845608028654
CUBIC = 0.044715
CHUNKS_PER_RELAY = 2
TILE = 256
MESH = pl.DeviceIdType.MESH


def dot_tn(left, right):
    return lax.dot_general(left, right, (((0,), (0,)), ((), ())), preferred_element_type=jnp.float32)


def gelu_slope(pre_act, tangent):
    return 0.5 * (1.0 + tangent) + 0.5 * pre_act * (1.0 - tangent * tangent) * GELU_C * (
        1.0 + 3.0 * CUBIC * pre_act * pre_act
    )


def gelu_parts(pre_act):
    tangent = jnp.tanh(GELU_C * (pre_act + CUBIC * pre_act * pre_act * pre_act))
    value = 0.5 * pre_act * (1.0 + tangent)
    return value.astype(jnp.bfloat16), gelu_slope(pre_act, tangent)


def norm_parts(x):
    xc = x - jnp.mean(x, axis=-1, keepdims=True)
    inverse = lax.rsqrt(jnp.mean(xc * xc, axis=-1, keepdims=True) + 1e-05)
    return xc * inverse, inverse


def kernel(
    segments,
    replicas,
    loss_scale,
    rising,
    falling,
    up_hbm,
    down_hbm,
    gain_hbm,
    out_up,
    out_down,
    out_gain,
    up,
    down,
    up_t,
    down_t,
    gain_ref,
    x_all,
    dy_all,
    y_out,
    dx_out,
    xh_st,
    inv_st,
    p_st,
    slope_st,
    a_st,
    t_st,
    da_st,
    n_all,
    p_all,
    slope_all,
    da_all,
    gain_acc,
    acc_up,
    acc_down,
    load_sem,
    feed_sem,
    fs_sem,
    bs_sem,
    xs_sem,
    xr_sem,
    ds_sem,
    dr_sem,
    gs_sem,
    gr_sem,
):
    place = lax.axis_index("segment")
    rep = lax.axis_index("dp")
    pair = place // 2
    core = place % 2
    last = segments // 2 - 1
    slots, chunks, rows, width = x_all.shape
    total = chunks * rows
    half = up.shape[1] // 2
    micro = rising.shape[0]
    local_rows = rising.shape[1] // 2
    mate = place + 1 - 2 * core
    slice_d = width // replicas
    per_chunk = rows // local_rows
    mine = pl.ds(pl.multiple_of(core * half, half), half)

    def feed_copy(which, m):
        flat = which * micro + m
        return pltpu.make_async_copy(
            (rising, falling)[which].at[
                m, pl.ds(pl.multiple_of(core * local_rows, local_rows), local_rows), :
            ],
            x_all.at[0, flat // per_chunk, pl.ds((flat % per_chunk) * local_rows, local_rows), :],
            feed_sem.at[flat],
        )

    load_gain = pltpu.make_async_copy(gain_hbm, gain_ref, load_sem.at[2])
    load_up = pltpu.make_async_copy(up_hbm.at[0], up, load_sem.at[0])
    load_down = pltpu.make_async_copy(down_hbm.at[0], down, load_sem.at[1])

    @pl.when(pair == 0)
    def _():
        for which in (0, 1):
            for m in range(micro):
                feed_copy(which, m).start()

    load_gain.start()
    load_up.start()
    load_down.start()

    peers = [(1, {"segment": mate})]
    for off in range(1, replicas):
        other = lax.rem(rep + off, replicas)
        peers.append((2 * off, {"dp": other}))
        peers.append((2 * off + 1, {"dp": other, "segment": mate}))

    barrier = pltpu.get_barrier_semaphore()

    @pl.when(pair > 0)
    def _():
        pl.semaphore_signal(barrier, inc=1, device_id={"segment": place - 2}, device_id_type=MESH)

    @pl.when(pair < last)
    def _():
        pl.semaphore_signal(barrier, inc=1, device_id={"segment": place + 2}, device_id_type=MESH)

    for _, peer in peers:
        pl.semaphore_signal(barrier, inc=1, device_id=peer, device_id_type=MESH)
    gain_acc[0] = jnp.zeros(gain_acc.shape[1:], gain_acc.dtype)
    pl.semaphore_wait(
        barrier,
        len(peers) + jnp.where(pair > 0, 1, 0) + jnp.where(pair < last, 1, 0),
    )

    def send(src, dst, send_sem, recv_sem, peer):
        return pltpu.make_async_remote_copy(
            src_ref=src,
            dst_ref=dst,
            send_sem=send_sem,
            recv_sem=recv_sem,
            device_id=peer,
            device_id_type=MESH,
        )

    def send_forward(i):
        return send(
            y_out.at[i], x_all.at[0, i], fs_sem.at[i], xr_sem.at[0, i], {"segment": place + 2}
        )

    def send_backward(i):
        return send(
            dx_out.at[i], dy_all.at[0, i], bs_sem.at[i], dr_sem.at[0, i], {"segment": place - 2}
        )

    def share(buf, sems, slot, i):
        if slot == 1:
            peer, origin = {"segment": mate}, 0
        elif slot % 2 == 0:
            peer, origin = {"dp": lax.rem(rep + slot // 2, replicas)}, 0
        else:
            peer, origin = {"segment": mate}, slot - 1
        return send(
            buf.at[origin, i], buf.at[slot, i], sems[0].at[slot, i], sems[1].at[slot, i], peer
        )

    xs = (xs_sem, xr_sem)
    ds = (ds_sem, dr_sem)

    def share_own(buf, sems, i):
        for off in range(1, replicas):
            share(buf, sems, 2 * off, i).start()
        share(buf, sems, 1, i).start()

    def hand_on(buf, sems, i):
        for off in range(1, replicas):
            share(buf, sems, 2 * off, i).wait_recv()
            share(buf, sems, 2 * off + 1, i).start()

    def span(i):
        return pl.ds(pl.multiple_of(i * rows, rows), rows)

    def slot_span(s):
        return pl.ds(pl.multiple_of(s * total, total), total)

    def transpose_weights():
        down_t[...] = down[...].T
        up_t[...] = up[...].T

    @pl.when(pair == 0)
    def _():
        for which in (0, 1):
            for m in range(micro):
                feed_copy(which, m).wait()

    load_gain.wait()
    load_up.wait()
    load_down.wait()
    gain_row = gain_ref[0:1, :]

    @pl.when(2 * pair > last)
    def _():
        transpose_weights()

    def forward(i, carry):
        @pl.when(pair > 0)
        def _():
            send_forward(i).wait_recv()

        x = x_all[0, i].astype(jnp.float32)
        xh, inverse = norm_parts(x)
        n = (xh * gain_row).astype(jnp.bfloat16)
        y = x
        for j in range(0, 2 * half, TILE):
            a = jnp.dot(n, up[:, j : j + TILE], preferred_element_type=jnp.float32)
            t = jnp.tanh(GELU_C * (a + CUBIC * a * a * a))
            p = (0.5 * a * (1.0 + t)).astype(jnp.bfloat16)
            a_st[:, j : j + TILE] = a
            t_st[:, j : j + TILE] = t
            p_st[span(i), j : j + TILE] = p
            y = y + jnp.dot(p, down[j : j + TILE, :], preferred_element_type=jnp.float32)
        y = y.astype(jnp.bfloat16)

        @pl.when(pair < last)
        def _():
            y_out[i] = y
            send_forward(i).start()

        @pl.when(pair == last)
        def _():
            dy_all[0, i] = (y.astype(jnp.float32) * loss_scale).astype(jnp.bfloat16)

        share_own(x_all, xs, i)

        @pl.when(i > 0)
        def _():
            hand_on(x_all, xs, i - 1)

        xh_st[i] = xh
        inv_st[i] = jnp.broadcast_to(inverse, (rows, 128))
        n_all[span(i), :] = n
        slope_st[i] = gelu_slope(a_st[...], t_st[...])
        return carry

    lax.fori_loop(0, chunks, forward, 0)
    hand_on(x_all, xs, chunks - 1)

    @pl.when(2 * pair <= last)
    def _():
        transpose_weights()

    def peers_forward():
        for s in range(1, slots, 2):
            for i in range(chunks):
                share(x_all, xs, s, i).wait_recv()

        def one(s, carry):
            xh, _ = norm_parts(x_all[s].reshape(total, width).astype(jnp.float32))
            n = (xh * gain_row).astype(jnp.bfloat16)
            n_all[slot_span(s), :] = n
            a = jnp.dot(n, up[:, mine], preferred_element_type=jnp.float32)
            p, slope = gelu_parts(a)
            p_all[slot_span(s), :] = p
            slope_all[slot_span(s), :] = slope
            return carry

        lax.fori_loop(1, slots, one, 0)
        p_all[slot_span(0), :] = p_st[:, mine]

    @pl.when(pair < last - 1)
    def _():
        peers_forward()

    def backward(i, carry):
        @pl.when(pair < last)
        def _():
            send_backward(i).wait_recv()

        @pl.when(pair == 0)
        def _():
            share_own(dy_all, ds, i)

        dy = dy_all[0, i]
        dn = jnp.zeros((rows, width), jnp.float32)
        for j in range(0, 2 * half, TILE):
            dp = jnp.dot(dy, down_t[:, j : j + TILE], preferred_element_type=jnp.float32)
            da = (dp * slope_st[i, :, j : j + TILE]).astype(jnp.bfloat16)
            da_st[span(i), j : j + TILE] = da
            dn = dn + jnp.dot(da, up_t[j : j + TILE, :], preferred_element_type=jnp.float32)
        xh = xh_st[i]
        e = dn * gain_row
        m1 = jnp.mean(e, axis=-1, keepdims=True)
        m2 = jnp.mean(e * xh, axis=-1, keepdims=True)
        inverse = inv_st[i][:, 0:1]
        dx = (dy.astype(jnp.float32) + inverse * (e - m1 - xh * m2)).astype(jnp.bfloat16)

        @pl.when(pair > 0)
        def _():
            dx_out[i] = dx
            send_backward(i).start()
            share_own(dy_all, ds, i)

        @pl.when(i > 0)
        def _():
            hand_on(dy_all, ds, i - 1)

        gain_acc[0] += jnp.sum((dn * xh).reshape(rows // 8, 8, width), axis=0)
        return carry

    lax.fori_loop(0, chunks, backward, 0)
    hand_on(dy_all, ds, chunks - 1)

    def send_gain(slot, peer):
        return send(gain_acc.at[0], gain_acc.at[slot], gs_sem.at[slot], gr_sem.at[slot], peer)

    for slot, peer in peers:
        send_gain(slot, peer).start()

    @pl.when(pair >= last - 1)
    def _():
        peers_forward()

    da_all[slot_span(0), :] = da_st[:, mine]
    for s in range(2, slots, 2):
        peer_da(s, slot_span, dy_all, down_t, mine, slope_all, da_all)
    for s in range(1, slots, 2):
        for i in range(chunks):
            share(dy_all, ds, s, i).wait_recv()
        peer_da(s, slot_span, dy_all, down_t, mine, slope_all, da_all)

    if slice_d % 128 == 0:
        cols = pl.ds(pl.multiple_of(rep * slice_d, slice_d), slice_d)
        out_up[...] = dot_tn(n_all[:, cols], da_all[...])
        dy_cols = dy_all[:, :, :, cols].reshape(slots * total, slice_d)
        out_down[...] = dot_tn(p_all[...], dy_cols)
    else:
        whole_up = dot_tn(n_all[...], da_all[...])
        whole_down = dot_tn(p_all[...], dy_all[...].reshape(slots * total, width))
        for j in range(replicas):
            acc_up[j] = whole_up[j * slice_d : (j + 1) * slice_d, :]
            acc_down[j] = whole_down[:, j * slice_d : (j + 1) * slice_d]
        out_up[...] = acc_up[rep]
        out_down[...] = acc_down[rep]

    gains = gain_acc[0]
    for slot, peer in peers:
        send_gain(slot, peer).wait()
        gains = gains + gain_acc[slot]
    gains = jnp.sum(gains, axis=0, keepdims=True)
    wide = out_gain.shape[1]
    for c in (0, 1):
        for j in range(replicas):
            start = c * (width // 2) + j * wide

            @pl.when((core == c) & (rep == j))
            def _():
                out_gain[...] = gains[:, start : start + wide]

    def drain(i, carry):
        for slot in range(1, slots):
            share(x_all, xs, slot, i).wait_send()
            share(dy_all, ds, slot, i).wait_send()

        @pl.when(pair < last)
        def _():
            send_forward(i).wait_send()

        @pl.when(pair > 0)
        def _():
            send_backward(i).wait_send()

        return carry

    lax.fori_loop(0, chunks, drain, 0)


def hand_over(*refs):
    sem = refs[6]
    copies = [pltpu.make_async_copy(refs[k], refs[3 + k], sem.at[k]) for k in range(3)]
    for copy in copies:
        copy.start()
    for copy in copies:
        copy.wait()


def peer_da(s, slot_span, dy_all, down_t, mine, slope_all, da_all):
    slots, chunks, rows, width = dy_all.shape
    dy = dy_all[s].reshape(chunks * rows, width)
    dp = jnp.dot(dy, down_t[:, mine], preferred_element_type=jnp.float32)
    da_all[slot_span(s), :] = (dp * slope_all[slot_span(s), :]).astype(jnp.bfloat16)


def body(feed_rising, feed_falling, up_weight, down_weight, norm_gain):
    segments = lax.axis_size("segment")
    replicas = lax.axis_size("dp")
    micro, rep_rows, width = feed_rising.shape
    local_rows = rep_rows // 2
    hidden = up_weight.shape[2]
    half = hidden // 2
    loss_scale = 1.0 / math.sqrt(2.0 * micro * rep_rows * replicas)
    chunks = 2 * CHUNKS_PER_RELAY
    rows = 2 * micro * local_rows // chunks
    total = chunks * rows
    slots = 2 * replicas
    slice_d = width // replicas
    bf16, f32 = jnp.bfloat16, jnp.float32
    vmem = pl.BlockSpec(memory_space=pltpu.VMEM)
    hbm = pl.BlockSpec(memory_space=pltpu.HBM)
    spare = (8, 128) if slice_d % 128 == 0 else None
    dma = pltpu.SemaphoreType.DMA
    grads = pl.pallas_call(
        functools.partial(kernel, segments, replicas, loss_scale),
        out_shape=(
            jax.ShapeDtypeStruct((slice_d, half), f32),
            jax.ShapeDtypeStruct((half, slice_d), f32),
            jax.ShapeDtypeStruct((1, width // 2 // replicas), f32),
        ),
        in_specs=[hbm, hbm, hbm, hbm, hbm],
        out_specs=(vmem, vmem, vmem),
        scratch_shapes=[
            pltpu.VMEM((width, hidden), bf16),
            pltpu.VMEM((hidden, width), bf16),
            pltpu.VMEM((hidden, width), bf16),
            pltpu.VMEM((width, hidden), bf16),
            pltpu.VMEM((norm_gain.shape[0], width), f32),
            pltpu.VMEM((slots, chunks, rows, width), bf16),
            pltpu.VMEM((slots, chunks, rows, width), bf16),
            pltpu.VMEM((chunks, rows, width), bf16),
            pltpu.VMEM((chunks, rows, width), bf16),
            pltpu.VMEM((chunks, rows, width), f32),
            pltpu.VMEM((chunks, rows, 128), f32),
            pltpu.VMEM((total, hidden), bf16),
            pltpu.VMEM((chunks, rows, hidden), f32),
            pltpu.VMEM((rows, hidden), f32),
            pltpu.VMEM((rows, hidden), f32),
            pltpu.VMEM((total, hidden), bf16),
            pltpu.VMEM((slots * total, width), bf16),
            pltpu.VMEM((slots * total, half), bf16),
            pltpu.VMEM((slots * total, half), f32),
            pltpu.VMEM((slots * total, half), bf16),
            pltpu.VMEM((slots, 8, width), f32),
            pltpu.VMEM(spare or (replicas, slice_d, half), f32),
            pltpu.VMEM(spare or (replicas, half, slice_d), f32),
            dma((3,)),
            dma((2 * micro,)),
            dma((chunks,)),
            dma((chunks,)),
            dma((slots, chunks)),
            dma((slots, chunks)),
            dma((slots, chunks)),
            dma((slots, chunks)),
            dma((slots,)),
            dma((slots,)),
        ],
        compiler_params=pltpu.CompilerParams(
            collective_id=0, has_side_effects=True, vmem_limit_bytes=60 * 1024 * 1024
        ),
        cost_estimate=pl.CostEstimate(
            flops=16 * total * width * hidden,
            bytes_accessed=6 * 1024 * 1024,
            transcendentals=3 * total * hidden,
        ),
        name="relay",
    )(feed_rising, feed_falling, up_weight, down_weight, norm_gain)
    return pl.pallas_call(
        hand_over,
        out_shape=tuple(jax.ShapeDtypeStruct(g.shape, g.dtype) for g in grads),
        in_specs=[hbm] * 3,
        out_specs=(hbm,) * 3,
        scratch_shapes=[dma((3,))],
        compiler_params=pltpu.CompilerParams(vmem_limit_bytes=60 * 1024 * 1024),
        name="hand_over",
    )(*grads)


def solution(mesh):
    return jax.shard_map(
        body,
        mesh=mesh,
        in_specs=(
            P(None, "dp", None),
            P(None, "dp", None),
            P("segment", None, None),
            P("segment", None, None),
            P("segment", None),
        ),
        out_specs=(P("dp", "segment"), P("segment", "dp"), P("segment", "dp")),
        check_vma=False,
    )
```

```python
import functools
import math

import jax
import jax.numpy as jnp
from jax import lax
from jax.experimental import pallas as pl
from jax.experimental.pallas import tpu as pltpu
from jax.sharding import PartitionSpec as P

GELU_C = 0.7978845608028654
CUBIC = 0.044715
CHUNKS_PER_RELAY = 4
LAG = 3
TILE = 256
MESH = pl.DeviceIdType.MESH


def dot_tn(left, right):
    return lax.dot_general(left, right, (((0,), (0,)), ((), ())), preferred_element_type=jnp.float32)


def gelu_slope(pre_act, tangent):
    return 0.5 * (1.0 + tangent) + 0.5 * pre_act * (1.0 - tangent * tangent) * GELU_C * (
        1.0 + 3.0 * CUBIC * pre_act * pre_act
    )


def gelu_parts(pre_act):
    tangent = jnp.tanh(GELU_C * (pre_act + CUBIC * pre_act * pre_act * pre_act))
    value = 0.5 * pre_act * (1.0 + tangent)
    return value.astype(jnp.bfloat16), gelu_slope(pre_act, tangent)


def norm_parts(x):
    xc = x - jnp.mean(x, axis=-1, keepdims=True)
    inverse = lax.rsqrt(jnp.mean(xc * xc, axis=-1, keepdims=True) + 1e-05)
    return xc * inverse, inverse


def kernel(
    segments,
    replicas,
    loss_scale,
    rising,
    falling,
    up_hbm,
    down_hbm,
    gain_hbm,
    out_up,
    out_down,
    out_gain,
    up,
    down,
    up_t,
    down_t,
    gain_ref,
    x_all,
    dy_all,
    y_out,
    dx_out,
    xh_st,
    inv_st,
    p_st,
    slope_st,
    a_st,
    t_st,
    da_st,
    n_all,
    p_all,
    slope_all,
    da_all,
    gain_acc,
    acc_up,
    acc_down,
    load_sem,
    feed_sem,
    fs_sem,
    bs_sem,
    xs_sem,
    xr_sem,
    ds_sem,
    dr_sem,
    gs_sem,
    gr_sem,
):
    place = lax.axis_index("segment")
    rep = lax.axis_index("dp")
    pair = place // 2
    core = place % 2
    last = segments // 2 - 1
    slots, chunks, rows, width = x_all.shape
    total = chunks * rows
    half = up.shape[1] // 2
    micro = rising.shape[0]
    local_rows = rising.shape[1] // 2
    mate = place + 1 - 2 * core
    slice_d = width // replicas
    per_chunk = rows // local_rows
    mine = pl.ds(pl.multiple_of(core * half, half), half)

    def feed_copy(which, m):
        flat = which * micro + m
        return pltpu.make_async_copy(
            (rising, falling)[which].at[
                m, pl.ds(pl.multiple_of(core * local_rows, local_rows), local_rows), :
            ],
            x_all.at[0, flat // per_chunk, pl.ds((flat % per_chunk) * local_rows, local_rows), :],
            feed_sem.at[flat],
        )

    load_gain = pltpu.make_async_copy(gain_hbm, gain_ref, load_sem.at[2])
    load_up = pltpu.make_async_copy(up_hbm.at[0], up, load_sem.at[0])
    load_down = pltpu.make_async_copy(down_hbm.at[0], down, load_sem.at[1])

    @pl.when(pair == 0)
    def _():
        for which in (0, 1):
            for m in range(micro):
                feed_copy(which, m).start()

    load_gain.start()
    load_up.start()
    load_down.start()

    peers = [(1, {"segment": mate})]
    for off in range(1, replicas):
        other = lax.rem(rep + off, replicas)
        peers.append((2 * off, {"dp": other}))
        peers.append((2 * off + 1, {"dp": other, "segment": mate}))

    barrier = pltpu.get_barrier_semaphore()

    @pl.when(pair > 0)
    def _():
        pl.semaphore_signal(barrier, inc=1, device_id={"segment": place - 2}, device_id_type=MESH)

    @pl.when(pair < last)
    def _():
        pl.semaphore_signal(barrier, inc=1, device_id={"segment": place + 2}, device_id_type=MESH)

    for _, peer in peers:
        pl.semaphore_signal(barrier, inc=1, device_id=peer, device_id_type=MESH)
    gain_acc[0] = jnp.zeros(gain_acc.shape[1:], gain_acc.dtype)
    pl.semaphore_wait(
        barrier,
        len(peers) + jnp.where(pair > 0, 1, 0) + jnp.where(pair < last, 1, 0),
    )

    def send(src, dst, send_sem, recv_sem, peer):
        return pltpu.make_async_remote_copy(
            src_ref=src,
            dst_ref=dst,
            send_sem=send_sem,
            recv_sem=recv_sem,
            device_id=peer,
            device_id_type=MESH,
        )

    def send_forward(i):
        return send(
            y_out.at[i], x_all.at[0, i], fs_sem.at[i], xr_sem.at[0, i], {"segment": place + 2}
        )

    def send_backward(i):
        return send(
            dx_out.at[i], dy_all.at[0, i], bs_sem.at[i], dr_sem.at[0, i], {"segment": place - 2}
        )

    def share(buf, sems, slot, i):
        if slot == 1:
            peer, origin = {"segment": mate}, 0
        elif slot % 2 == 0:
            peer, origin = {"dp": lax.rem(rep + slot // 2, replicas)}, 0
        else:
            peer, origin = {"segment": mate}, slot - 1
        return send(
            buf.at[origin, i], buf.at[slot, i], sems[0].at[slot, i], sems[1].at[slot, i], peer
        )

    xs = (xs_sem, xr_sem)
    ds = (ds_sem, dr_sem)

    def share_own(buf, sems, i):
        for off in range(1, replicas):
            share(buf, sems, 2 * off, i).start()
        share(buf, sems, 1, i).start()

    def hand_on(buf, sems, i):
        for off in range(1, replicas):
            share(buf, sems, 2 * off, i).wait_recv()
            share(buf, sems, 2 * off + 1, i).start()

    def span(i):
        return pl.ds(pl.multiple_of(i * rows, rows), rows)

    def slot_span(s):
        return pl.ds(pl.multiple_of(s * total, total), total)

    def transpose_weights():
        down_t[...] = down[...].T
        up_t[...] = up[...].T

    @pl.when(pair == 0)
    def _():
        for which in (0, 1):
            for m in range(micro):
                feed_copy(which, m).wait()

    load_gain.wait()
    load_up.wait()
    load_down.wait()
    gain_row = gain_ref[0:1, :]

    @pl.when(2 * pair > last)
    def _():
        transpose_weights()

    def forward(i, carry):
        @pl.when(pair > 0)
        def _():
            send_forward(i).wait_recv()

        x = x_all[0, i].astype(jnp.float32)
        xh, inverse = norm_parts(x)
        n = (xh * gain_row).astype(jnp.bfloat16)
        y = x
        for j in range(0, 2 * half, TILE):
            a = jnp.dot(n, up[:, j : j + TILE], preferred_element_type=jnp.float32)
            t = jnp.tanh(GELU_C * (a + CUBIC * a * a * a))
            p = (0.5 * a * (1.0 + t)).astype(jnp.bfloat16)
            a_st[:, j : j + TILE] = a
            t_st[:, j : j + TILE] = t
            p_st[span(i), j : j + TILE] = p
            y = y + jnp.dot(p, down[j : j + TILE, :], preferred_element_type=jnp.float32)
        y = y.astype(jnp.bfloat16)

        @pl.when(pair < last)
        def _():
            y_out[i] = y
            send_forward(i).start()

        @pl.when(pair == last)
        def _():
            dy_all[0, i] = (y.astype(jnp.float32) * loss_scale).astype(jnp.bfloat16)

        share_own(x_all, xs, i)

        xh_st[i] = xh
        inv_st[i] = jnp.broadcast_to(inverse, (rows, 128))
        n_all[span(i), :] = n
        slope_st[i] = gelu_slope(a_st[...], t_st[...])
        return carry

    lax.fori_loop(0, chunks, forward, 0)

    def hand_on_rows(i, carry):
        hand_on(x_all, xs, i)
        return carry

    lax.fori_loop(0, chunks, hand_on_rows, 0)

    @pl.when(2 * pair <= last)
    def _():
        transpose_weights()

    def peers_forward():
        for s in range(1, slots, 2):
            for i in range(chunks):
                share(x_all, xs, s, i).wait_recv()

        def one(s, carry):
            xh, _ = norm_parts(x_all[s].reshape(total, width).astype(jnp.float32))
            n = (xh * gain_row).astype(jnp.bfloat16)
            n_all[slot_span(s), :] = n
            a = jnp.dot(n, up[:, mine], preferred_element_type=jnp.float32)
            p, slope = gelu_parts(a)
            p_all[slot_span(s), :] = p
            slope_all[slot_span(s), :] = slope
            return carry

        lax.fori_loop(1, slots, one, 0)
        p_all[slot_span(0), :] = p_st[:, mine]

    @pl.when(pair < last - 1)
    def _():
        peers_forward()

    def backward(i, carry):
        @pl.when(pair < last)
        def _():
            send_backward(i).wait_recv()

        @pl.when(pair == 0)
        def _():
            share_own(dy_all, ds, i)

        dy = dy_all[0, i]
        dn = jnp.zeros((rows, width), jnp.float32)
        for j in range(0, 2 * half, TILE):
            dp = jnp.dot(dy, down_t[:, j : j + TILE], preferred_element_type=jnp.float32)
            da = (dp * slope_st[i, :, j : j + TILE]).astype(jnp.bfloat16)
            da_st[span(i), j : j + TILE] = da
            dn = dn + jnp.dot(da, up_t[j : j + TILE, :], preferred_element_type=jnp.float32)
        xh = xh_st[i]
        e = dn * gain_row
        m1 = jnp.mean(e, axis=-1, keepdims=True)
        m2 = jnp.mean(e * xh, axis=-1, keepdims=True)
        inverse = inv_st[i][:, 0:1]
        dx = (dy.astype(jnp.float32) + inverse * (e - m1 - xh * m2)).astype(jnp.bfloat16)

        @pl.when(pair > 0)
        def _():
            dx_out[i] = dx
            send_backward(i).start()
            share_own(dy_all, ds, i)

        @pl.when(i >= LAG)
        def _():
            hand_on(dy_all, ds, i - LAG)

        gain_acc[0] += jnp.sum((dn * xh).reshape(rows // 8, 8, width), axis=0)
        return carry

    lax.fori_loop(0, chunks, backward, 0)
    for i in range(chunks - LAG, chunks):
        hand_on(dy_all, ds, i)

    def send_gain(slot, peer):
        return send(gain_acc.at[0], gain_acc.at[slot], gs_sem.at[slot], gr_sem.at[slot], peer)

    for slot, peer in peers:
        send_gain(slot, peer).start()

    @pl.when(pair >= last - 1)
    def _():
        peers_forward()

    da_all[slot_span(0), :] = da_st[:, mine]
    for s in range(2, slots, 2):
        peer_da(s, slot_span, dy_all, down_t, mine, slope_all, da_all)
    for s in range(1, slots, 2):
        for i in range(chunks):
            share(dy_all, ds, s, i).wait_recv()
        peer_da(s, slot_span, dy_all, down_t, mine, slope_all, da_all)

    if slice_d % 128 == 0:
        cols = pl.ds(pl.multiple_of(rep * slice_d, slice_d), slice_d)
        out_up[...] = dot_tn(n_all[:, cols], da_all[...])
        dy_cols = dy_all[:, :, :, cols].reshape(slots * total, slice_d)
        out_down[...] = dot_tn(p_all[...], dy_cols)
    else:
        whole_up = dot_tn(n_all[...], da_all[...])
        whole_down = dot_tn(p_all[...], dy_all[...].reshape(slots * total, width))
        for j in range(replicas):
            acc_up[j] = whole_up[j * slice_d : (j + 1) * slice_d, :]
            acc_down[j] = whole_down[:, j * slice_d : (j + 1) * slice_d]
        out_up[...] = acc_up[rep]
        out_down[...] = acc_down[rep]

    gains = gain_acc[0]
    for slot, peer in peers:
        send_gain(slot, peer).wait()
        gains = gains + gain_acc[slot]
    gains = jnp.sum(gains, axis=0, keepdims=True)
    wide = out_gain.shape[1]
    for c in (0, 1):
        for j in range(replicas):
            start = c * (width // 2) + j * wide

            @pl.when((core == c) & (rep == j))
            def _():
                out_gain[...] = gains[:, start : start + wide]

    def drain(i, carry):
        for slot in range(1, slots):
            share(x_all, xs, slot, i).wait_send()
            share(dy_all, ds, slot, i).wait_send()

        @pl.when(pair < last)
        def _():
            send_forward(i).wait_send()

        @pl.when(pair > 0)
        def _():
            send_backward(i).wait_send()

        return carry

    lax.fori_loop(0, chunks, drain, 0)


def hand_over(*refs):
    for k in range(3):
        refs[3 + k][...] = refs[k][...]


def peer_da(s, slot_span, dy_all, down_t, mine, slope_all, da_all):
    slots, chunks, rows, width = dy_all.shape
    dy = dy_all[s].reshape(chunks * rows, width)
    dp = jnp.dot(dy, down_t[:, mine], preferred_element_type=jnp.float32)
    da_all[slot_span(s), :] = (dp * slope_all[slot_span(s), :]).astype(jnp.bfloat16)


def body(feed_rising, feed_falling, up_weight, down_weight, norm_gain):
    segments = lax.axis_size("segment")
    replicas = lax.axis_size("dp")
    micro, rep_rows, width = feed_rising.shape
    local_rows = rep_rows // 2
    hidden = up_weight.shape[2]
    half = hidden // 2
    loss_scale = 1.0 / math.sqrt(2.0 * micro * rep_rows * replicas)
    chunks = 2 * CHUNKS_PER_RELAY
    rows = 2 * micro * local_rows // chunks
    total = chunks * rows
    slots = 2 * replicas
    slice_d = width // replicas
    bf16, f32 = jnp.bfloat16, jnp.float32
    vmem = pl.BlockSpec(memory_space=pltpu.VMEM)
    hbm = pl.BlockSpec(memory_space=pltpu.HBM)
    spare = (8, 128) if slice_d % 128 == 0 else None
    dma = pltpu.SemaphoreType.DMA
    grads = pl.pallas_call(
        functools.partial(kernel, segments, replicas, loss_scale),
        out_shape=(
            jax.ShapeDtypeStruct((slice_d, half), f32),
            jax.ShapeDtypeStruct((half, slice_d), f32),
            jax.ShapeDtypeStruct((1, width // 2 // replicas), f32),
        ),
        in_specs=[hbm, hbm, hbm, hbm, hbm],
        out_specs=(vmem, vmem, vmem),
        scratch_shapes=[
            pltpu.VMEM((width, hidden), bf16),
            pltpu.VMEM((hidden, width), bf16),
            pltpu.VMEM((hidden, width), bf16),
            pltpu.VMEM((width, hidden), bf16),
            pltpu.VMEM((norm_gain.shape[0], width), f32),
            pltpu.VMEM((slots, chunks, rows, width), bf16),
            pltpu.VMEM((slots, chunks, rows, width), bf16),
            pltpu.VMEM((chunks, rows, width), bf16),
            pltpu.VMEM((chunks, rows, width), bf16),
            pltpu.VMEM((chunks, rows, width), f32),
            pltpu.VMEM((chunks, rows, 128), f32),
            pltpu.VMEM((total, hidden), bf16),
            pltpu.VMEM((chunks, rows, hidden), f32),
            pltpu.VMEM((rows, hidden), f32),
            pltpu.VMEM((rows, hidden), f32),
            pltpu.VMEM((total, hidden), bf16),
            pltpu.VMEM((slots * total, width), bf16),
            pltpu.VMEM((slots * total, half), bf16),
            pltpu.VMEM((slots * total, half), f32),
            pltpu.VMEM((slots * total, half), bf16),
            pltpu.VMEM((slots, 8, width), f32),
            pltpu.VMEM(spare or (replicas, slice_d, half), f32),
            pltpu.VMEM(spare or (replicas, half, slice_d), f32),
            dma((3,)),
            dma((2 * micro,)),
            dma((chunks,)),
            dma((chunks,)),
            dma((slots, chunks)),
            dma((slots, chunks)),
            dma((slots, chunks)),
            dma((slots, chunks)),
            dma((slots,)),
            dma((slots,)),
        ],
        compiler_params=pltpu.CompilerParams(
            collective_id=0, has_side_effects=True, vmem_limit_bytes=60 * 1024 * 1024
        ),
        cost_estimate=pl.CostEstimate(
            flops=16 * total * width * hidden,
            bytes_accessed=6 * 1024 * 1024,
            transcendentals=3 * total * hidden,
        ),
        name="relay",
    )(feed_rising, feed_falling, up_weight, down_weight, norm_gain)
    return pl.pallas_call(
        hand_over,
        out_shape=tuple(jax.ShapeDtypeStruct(g.shape, g.dtype) for g in grads),
        in_specs=[vmem] * 3,
        out_specs=(vmem,) * 3,
        name="hand_over",
    )(*grads)


def solution(mesh):
    return jax.shard_map(
        body,
        mesh=mesh,
        in_specs=(
            P(None, "dp", None),
            P(None, "dp", None),
            P("segment", None, None),
            P("segment", None, None),
            P("segment", None),
        ),
        out_specs=(P("dp", "segment"), P("segment", "dp"), P("segment", "dp")),
        check_vma=False,
    )
```

```python
import functools
import math

import jax
import jax.numpy as jnp
from jax import lax
from jax.experimental import pallas as pl
from jax.experimental.pallas import tpu as pltpu
from jax.sharding import PartitionSpec as P

GELU_C = 0.7978845608028654
CUBIC = 0.044715
CHUNKS_PER_RELAY = 4
LAG = 3
TILE = 256
MESH = pl.DeviceIdType.MESH


def dot_tn(left, right):
    return lax.dot_general(left, right, (((0,), (0,)), ((), ())), preferred_element_type=jnp.float32)


def gelu_slope(pre_act, tangent):
    return 0.5 * (1.0 + tangent) + 0.5 * pre_act * (1.0 - tangent * tangent) * GELU_C * (
        1.0 + 3.0 * CUBIC * pre_act * pre_act
    )


def gelu_parts(pre_act):
    tangent = jnp.tanh(GELU_C * (pre_act + CUBIC * pre_act * pre_act * pre_act))
    value = 0.5 * pre_act * (1.0 + tangent)
    return value.astype(jnp.bfloat16), gelu_slope(pre_act, tangent)


def norm_parts(x):
    xc = x - jnp.mean(x, axis=-1, keepdims=True)
    inverse = lax.rsqrt(jnp.mean(xc * xc, axis=-1, keepdims=True) + 1e-05)
    return xc * inverse, inverse


def kernel(
    segments,
    replicas,
    loss_scale,
    rising,
    falling,
    up_hbm,
    down_hbm,
    gain_hbm,
    out_up,
    out_down,
    out_gain,
    up,
    down,
    up_t,
    down_t,
    gain_ref,
    x_all,
    dy_all,
    y_out,
    dx_out,
    xh_st,
    inv_st,
    p_st,
    slope_st,
    a_st,
    t_st,
    da_st,
    n_all,
    p_all,
    slope_all,
    da_all,
    gain_acc,
    acc_up,
    acc_down,
    load_sem,
    feed_sem,
    fs_sem,
    bs_sem,
    xs_sem,
    xr_sem,
    ds_sem,
    dr_sem,
    gs_sem,
    gr_sem,
):
    place = lax.axis_index("segment")
    rep = lax.axis_index("dp")
    pair = place // 2
    core = place % 2
    last = segments // 2 - 1
    slots, chunks, rows, width = x_all.shape
    total = chunks * rows
    half = up.shape[1] // 2
    micro = rising.shape[0]
    local_rows = rising.shape[1] // 2
    mate = place + 1 - 2 * core
    slice_d = width // replicas
    per_chunk = rows // local_rows
    mine = pl.ds(pl.multiple_of(core * half, half), half)

    def feed_copy(which, m):
        flat = which * micro + m
        return pltpu.make_async_copy(
            (rising, falling)[which].at[
                m, pl.ds(pl.multiple_of(core * local_rows, local_rows), local_rows), :
            ],
            x_all.at[0, flat // per_chunk, pl.ds((flat % per_chunk) * local_rows, local_rows), :],
            feed_sem.at[flat],
        )

    load_gain = pltpu.make_async_copy(gain_hbm, gain_ref, load_sem.at[2])
    load_up = pltpu.make_async_copy(up_hbm.at[0], up, load_sem.at[0])
    load_down = pltpu.make_async_copy(down_hbm.at[0], down, load_sem.at[1])

    @pl.when(pair == 0)
    def _():
        for which in (0, 1):
            for m in range(micro):
                feed_copy(which, m).start()

    load_gain.start()
    load_up.start()
    load_down.start()

    peers = [(1, {"segment": mate})]
    for off in range(1, replicas):
        other = lax.rem(rep + off, replicas)
        peers.append((2 * off, {"dp": other}))
        peers.append((2 * off + 1, {"dp": other, "segment": mate}))

    barrier = pltpu.get_barrier_semaphore()

    @pl.when(pair > 0)
    def _():
        pl.semaphore_signal(barrier, inc=1, device_id={"segment": place - 2}, device_id_type=MESH)

    @pl.when(pair < last)
    def _():
        pl.semaphore_signal(barrier, inc=1, device_id={"segment": place + 2}, device_id_type=MESH)

    for _, peer in peers:
        pl.semaphore_signal(barrier, inc=1, device_id=peer, device_id_type=MESH)
    gain_acc[0] = jnp.zeros(gain_acc.shape[1:], gain_acc.dtype)
    pl.semaphore_wait(
        barrier,
        len(peers) + jnp.where(pair > 0, 1, 0) + jnp.where(pair < last, 1, 0),
    )

    def send(src, dst, send_sem, recv_sem, peer):
        return pltpu.make_async_remote_copy(
            src_ref=src,
            dst_ref=dst,
            send_sem=send_sem,
            recv_sem=recv_sem,
            device_id=peer,
            device_id_type=MESH,
        )

    def send_forward(i):
        return send(
            y_out.at[i], x_all.at[0, i], fs_sem.at[i], xr_sem.at[0, i], {"segment": place + 2}
        )

    def send_backward(i):
        return send(
            dx_out.at[i], dy_all.at[0, i], bs_sem.at[i], dr_sem.at[0, i], {"segment": place - 2}
        )

    def share(buf, sems, slot, i):
        if slot == 1:
            peer, origin = {"segment": mate}, 0
        elif slot % 2 == 0:
            peer, origin = {"dp": lax.rem(rep + slot // 2, replicas)}, 0
        else:
            peer, origin = {"segment": mate}, slot - 1
        return send(
            buf.at[origin, i], buf.at[slot, i], sems[0].at[slot, i], sems[1].at[slot, i], peer
        )

    xs = (xs_sem, xr_sem)
    ds = (ds_sem, dr_sem)

    def share_own(buf, sems, i):
        for off in range(1, replicas):
            share(buf, sems, 2 * off, i).start()
        share(buf, sems, 1, i).start()

    def hand_on(buf, sems, i):
        for off in range(1, replicas):
            share(buf, sems, 2 * off, i).wait_recv()
            share(buf, sems, 2 * off + 1, i).start()

    def span(i):
        return pl.ds(pl.multiple_of(i * rows, rows), rows)

    def slot_span(s):
        return pl.ds(pl.multiple_of(s * total, total), total)

    def transpose_weights():
        down_t[...] = down[...].T
        up_t[...] = up[...].T

    @pl.when(pair == 0)
    def _():
        for which in (0, 1):
            for m in range(micro):
                feed_copy(which, m).wait()

    load_gain.wait()
    load_up.wait()
    load_down.wait()
    gain_row = gain_ref[0:1, :]

    @pl.when(2 * pair > last)
    def _():
        transpose_weights()

    def forward(i, carry):
        @pl.when(pair > 0)
        def _():
            send_forward(i).wait_recv()

        x = x_all[0, i].astype(jnp.float32)
        xh, inverse = norm_parts(x)
        n = (xh * gain_row).astype(jnp.bfloat16)
        y = x
        for j in range(0, 2 * half, TILE):
            a = jnp.dot(n, up[:, j : j + TILE], preferred_element_type=jnp.float32)
            t = jnp.tanh(GELU_C * (a + CUBIC * a * a * a))
            p = (0.5 * a * (1.0 + t)).astype(jnp.bfloat16)
            a_st[:, j : j + TILE] = a
            t_st[:, j : j + TILE] = t
            p_st[span(i), j : j + TILE] = p
            y = y + jnp.dot(p, down[j : j + TILE, :], preferred_element_type=jnp.float32)
        y = y.astype(jnp.bfloat16)

        @pl.when(pair < last)
        def _():
            y_out[i] = y
            send_forward(i).start()

        @pl.when(pair == last)
        def _():
            dy_all[0, i] = (y.astype(jnp.float32) * loss_scale).astype(jnp.bfloat16)

        xh_st[i] = xh
        inv_st[i] = jnp.broadcast_to(inverse, (rows, 128))
        n_all[span(i), :] = n
        slope_st[i] = gelu_slope(a_st[...], t_st[...])
        return carry

    lax.fori_loop(0, chunks, forward, 0)

    @pl.when(2 * pair <= last)
    def _():
        transpose_weights()

    def share_rows(buf, sems):
        def share_chunk(i, carry):
            share_own(buf, sems, i)
            return carry

        def hand_on_chunk(i, carry):
            hand_on(buf, sems, i)
            return carry

        lax.fori_loop(0, chunks, share_chunk, 0)
        lax.fori_loop(0, chunks, hand_on_chunk, 0)

    def peers_forward():
        share_rows(x_all, xs)
        for s in range(1, slots, 2):
            for i in range(chunks):
                share(x_all, xs, s, i).wait_recv()

        def one(s, carry):
            xh, _ = norm_parts(x_all[s].reshape(total, width).astype(jnp.float32))
            n = (xh * gain_row).astype(jnp.bfloat16)
            n_all[slot_span(s), :] = n
            a = jnp.dot(n, up[:, mine], preferred_element_type=jnp.float32)
            p, slope = gelu_parts(a)
            p_all[slot_span(s), :] = p
            slope_all[slot_span(s), :] = slope
            return carry

        lax.fori_loop(1, slots, one, 0)
        p_all[slot_span(0), :] = p_st[:, mine]

    @pl.when(pair < last - 1)
    def _():
        peers_forward()

    def backward(i, carry):
        @pl.when(pair < last)
        def _():
            send_backward(i).wait_recv()

        @pl.when(pair == 0)
        def _():
            share_own(dy_all, ds, i)

        dy = dy_all[0, i]
        dn = jnp.zeros((rows, width), jnp.float32)
        for j in range(0, 2 * half, TILE):
            dp = jnp.dot(dy, down_t[:, j : j + TILE], preferred_element_type=jnp.float32)
            da = (dp * slope_st[i, :, j : j + TILE]).astype(jnp.bfloat16)
            da_st[span(i), j : j + TILE] = da
            dn = dn + jnp.dot(da, up_t[j : j + TILE, :], preferred_element_type=jnp.float32)
        xh = xh_st[i]
        e = dn * gain_row
        m1 = jnp.mean(e, axis=-1, keepdims=True)
        m2 = jnp.mean(e * xh, axis=-1, keepdims=True)
        inverse = inv_st[i][:, 0:1]
        dx = (dy.astype(jnp.float32) + inverse * (e - m1 - xh * m2)).astype(jnp.bfloat16)

        @pl.when(pair > 0)
        def _():
            dx_out[i] = dx
            send_backward(i).start()

        @pl.when((pair == 0) & (i >= LAG))
        def _():
            hand_on(dy_all, ds, i - LAG)

        gain_acc[0] += jnp.sum((dn * xh).reshape(rows // 8, 8, width), axis=0)
        return carry

    lax.fori_loop(0, chunks, backward, 0)
    @pl.when(pair == 0)
    def _():
        for i in range(chunks - LAG, chunks):
            hand_on(dy_all, ds, i)

    @pl.when(pair > 0)
    def _():
        share_rows(dy_all, ds)

    def send_gain(slot, peer):
        return send(gain_acc.at[0], gain_acc.at[slot], gs_sem.at[slot], gr_sem.at[slot], peer)

    for slot, peer in peers:
        send_gain(slot, peer).start()

    @pl.when(pair >= last - 1)
    def _():
        peers_forward()

    da_all[slot_span(0), :] = da_st[:, mine]
    for s in range(2, slots, 2):
        peer_da(s, slot_span, dy_all, down_t, mine, slope_all, da_all)
    for s in range(1, slots, 2):
        for i in range(chunks):
            share(dy_all, ds, s, i).wait_recv()
        peer_da(s, slot_span, dy_all, down_t, mine, slope_all, da_all)

    if slice_d % 128 == 0:
        cols = pl.ds(pl.multiple_of(rep * slice_d, slice_d), slice_d)
        out_up[...] = dot_tn(n_all[:, cols], da_all[...])
        dy_cols = dy_all[:, :, :, cols].reshape(slots * total, slice_d)
        out_down[...] = dot_tn(p_all[...], dy_cols)
    else:
        whole_up = dot_tn(n_all[...], da_all[...])
        whole_down = dot_tn(p_all[...], dy_all[...].reshape(slots * total, width))
        for j in range(replicas):
            acc_up[j] = whole_up[j * slice_d : (j + 1) * slice_d, :]
            acc_down[j] = whole_down[:, j * slice_d : (j + 1) * slice_d]
        out_up[...] = acc_up[rep]
        out_down[...] = acc_down[rep]

    gains = gain_acc[0]
    for slot, peer in peers:
        send_gain(slot, peer).wait()
        gains = gains + gain_acc[slot]
    gains = jnp.sum(gains, axis=0, keepdims=True)
    wide = out_gain.shape[1]
    for c in (0, 1):
        for j in range(replicas):
            start = c * (width // 2) + j * wide

            @pl.when((core == c) & (rep == j))
            def _():
                out_gain[...] = gains[:, start : start + wide]

    def drain(i, carry):
        for slot in range(1, slots):
            share(x_all, xs, slot, i).wait_send()
            share(dy_all, ds, slot, i).wait_send()

        @pl.when(pair < last)
        def _():
            send_forward(i).wait_send()

        @pl.when(pair > 0)
        def _():
            send_backward(i).wait_send()

        return carry

    lax.fori_loop(0, chunks, drain, 0)


def hand_over(*refs):
    for k in range(3):
        refs[3 + k][...] = refs[k][...]


def peer_da(s, slot_span, dy_all, down_t, mine, slope_all, da_all):
    slots, chunks, rows, width = dy_all.shape
    dy = dy_all[s].reshape(chunks * rows, width)
    dp = jnp.dot(dy, down_t[:, mine], preferred_element_type=jnp.float32)
    da_all[slot_span(s), :] = (dp * slope_all[slot_span(s), :]).astype(jnp.bfloat16)


def body(feed_rising, feed_falling, up_weight, down_weight, norm_gain):
    segments = lax.axis_size("segment")
    replicas = lax.axis_size("dp")
    micro, rep_rows, width = feed_rising.shape
    local_rows = rep_rows // 2
    hidden = up_weight.shape[2]
    half = hidden // 2
    loss_scale = 1.0 / math.sqrt(2.0 * micro * rep_rows * replicas)
    chunks = 2 * CHUNKS_PER_RELAY
    rows = 2 * micro * local_rows // chunks
    total = chunks * rows
    slots = 2 * replicas
    slice_d = width // replicas
    bf16, f32 = jnp.bfloat16, jnp.float32
    vmem = pl.BlockSpec(memory_space=pltpu.VMEM)
    hbm = pl.BlockSpec(memory_space=pltpu.HBM)
    spare = (8, 128) if slice_d % 128 == 0 else None
    dma = pltpu.SemaphoreType.DMA
    grads = pl.pallas_call(
        functools.partial(kernel, segments, replicas, loss_scale),
        out_shape=(
            jax.ShapeDtypeStruct((slice_d, half), f32),
            jax.ShapeDtypeStruct((half, slice_d), f32),
            jax.ShapeDtypeStruct((1, width // 2 // replicas), f32),
        ),
        in_specs=[hbm, hbm, hbm, hbm, hbm],
        out_specs=(vmem, vmem, vmem),
        scratch_shapes=[
            pltpu.VMEM((width, hidden), bf16),
            pltpu.VMEM((hidden, width), bf16),
            pltpu.VMEM((hidden, width), bf16),
            pltpu.VMEM((width, hidden), bf16),
            pltpu.VMEM((norm_gain.shape[0], width), f32),
            pltpu.VMEM((slots, chunks, rows, width), bf16),
            pltpu.VMEM((slots, chunks, rows, width), bf16),
            pltpu.VMEM((chunks, rows, width), bf16),
            pltpu.VMEM((chunks, rows, width), bf16),
            pltpu.VMEM((chunks, rows, width), f32),
            pltpu.VMEM((chunks, rows, 128), f32),
            pltpu.VMEM((total, hidden), bf16),
            pltpu.VMEM((chunks, rows, hidden), f32),
            pltpu.VMEM((rows, hidden), f32),
            pltpu.VMEM((rows, hidden), f32),
            pltpu.VMEM((total, hidden), bf16),
            pltpu.VMEM((slots * total, width), bf16),
            pltpu.VMEM((slots * total, half), bf16),
            pltpu.VMEM((slots * total, half), f32),
            pltpu.VMEM((slots * total, half), bf16),
            pltpu.VMEM((slots, 8, width), f32),
            pltpu.VMEM(spare or (replicas, slice_d, half), f32),
            pltpu.VMEM(spare or (replicas, half, slice_d), f32),
            dma((3,)),
            dma((2 * micro,)),
            dma((chunks,)),
            dma((chunks,)),
            dma((slots, chunks)),
            dma((slots, chunks)),
            dma((slots, chunks)),
            dma((slots, chunks)),
            dma((slots,)),
            dma((slots,)),
        ],
        compiler_params=pltpu.CompilerParams(
            collective_id=0, has_side_effects=True, vmem_limit_bytes=60 * 1024 * 1024
        ),
        cost_estimate=pl.CostEstimate(
            flops=16 * total * width * hidden,
            bytes_accessed=6 * 1024 * 1024,
            transcendentals=3 * total * hidden,
        ),
        name="relay",
    )(feed_rising, feed_falling, up_weight, down_weight, norm_gain)
    return pl.pallas_call(
        hand_over,
        out_shape=tuple(jax.ShapeDtypeStruct(g.shape, g.dtype) for g in grads),
        in_specs=[vmem] * 3,
        out_specs=(vmem,) * 3,
        name="hand_over",
    )(*grads)


def solution(mesh):
    return jax.shard_map(
        body,
        mesh=mesh,
        in_specs=(
            P(None, "dp", None),
            P(None, "dp", None),
            P("segment", None, None),
            P("segment", None, None),
            P("segment", None),
        ),
        out_specs=(P("dp", "segment"), P("segment", "dp"), P("segment", "dp")),
        check_vma=False,
    )
```

```python
import functools
import math

import jax
import jax.numpy as jnp
from jax import lax
from jax.experimental import pallas as pl
from jax.experimental.pallas import tpu as pltpu
from jax.sharding import PartitionSpec as P

GELU_C = 0.7978845608028654
CUBIC = 0.044715
CHUNKS_PER_RELAY = 4
LAG = 3
TILE = 256
MESH = pl.DeviceIdType.MESH


def dot_tn(left, right):
    return lax.dot_general(left, right, (((0,), (0,)), ((), ())), preferred_element_type=jnp.float32)


def gelu_slope(pre_act, tangent):
    return 0.5 * (1.0 + tangent) + 0.5 * pre_act * (1.0 - tangent * tangent) * GELU_C * (
        1.0 + 3.0 * CUBIC * pre_act * pre_act
    )


def gelu_parts(pre_act):
    tangent = jnp.tanh(GELU_C * (pre_act + CUBIC * pre_act * pre_act * pre_act))
    value = 0.5 * pre_act * (1.0 + tangent)
    return value.astype(jnp.bfloat16), gelu_slope(pre_act, tangent)


def norm_parts(x):
    xc = x - jnp.mean(x, axis=-1, keepdims=True)
    inverse = lax.rsqrt(jnp.mean(xc * xc, axis=-1, keepdims=True) + 1e-05)
    return xc * inverse, inverse


def kernel(
    segments,
    replicas,
    loss_scale,
    rising,
    falling,
    up_hbm,
    down_hbm,
    gain_hbm,
    out_up,
    out_down,
    out_gain,
    up,
    down,
    up_t,
    down_t,
    gain_ref,
    x_all,
    dy_all,
    y_out,
    dx_out,
    xh_st,
    inv_st,
    p_st,
    slope_st,
    a_st,
    t_st,
    da_st,
    n_all,
    p_all,
    slope_all,
    da_all,
    gain_acc,
    acc_up,
    acc_down,
    load_sem,
    feed_sem,
    fs_sem,
    bs_sem,
    ac_sem,
    xs_sem,
    xr_sem,
    ds_sem,
    dr_sem,
    gs_sem,
    gr_sem,
):
    place = lax.axis_index("segment")
    rep = lax.axis_index("dp")
    pair = place // 2
    core = place % 2
    last = segments // 2 - 1
    slots, chunks, rows, width = x_all.shape
    total = chunks * rows
    half = up.shape[1] // 2
    micro = rising.shape[0]
    local_rows = rising.shape[1] // 2
    mate = place + 1 - 2 * core
    slice_d = width // replicas
    per_chunk = rows // local_rows
    mine = pl.ds(pl.multiple_of(core * half, half), half)

    def feed_copy(which, m):
        flat = which * micro + m
        return pltpu.make_async_copy(
            (rising, falling)[which].at[
                m, pl.ds(pl.multiple_of(core * local_rows, local_rows), local_rows), :
            ],
            x_all.at[0, flat // per_chunk, pl.ds((flat % per_chunk) * local_rows, local_rows), :],
            feed_sem.at[flat],
        )

    load_gain = pltpu.make_async_copy(gain_hbm, gain_ref, load_sem.at[2])
    load_up = pltpu.make_async_copy(up_hbm.at[0], up, load_sem.at[0])
    load_down = pltpu.make_async_copy(down_hbm.at[0], down, load_sem.at[1])

    @pl.when(pair == 0)
    def _():
        for which in (0, 1):
            for m in range(micro):
                feed_copy(which, m).start()

    load_gain.start()
    load_up.start()
    load_down.start()

    peers = [(1, {"segment": mate})]
    for off in range(1, replicas):
        other = lax.rem(rep + off, replicas)
        peers.append((2 * off, {"dp": other}))
        peers.append((2 * off + 1, {"dp": other, "segment": mate}))

    barrier = pltpu.get_barrier_semaphore()

    @pl.when(pair > 0)
    def _():
        pl.semaphore_signal(barrier, inc=1, device_id={"segment": place - 2}, device_id_type=MESH)

    @pl.when(pair < last)
    def _():
        pl.semaphore_signal(barrier, inc=1, device_id={"segment": place + 2}, device_id_type=MESH)

    for off in range(1, replicas):
        other = lax.rem(rep + off, replicas)

        @pl.when(pair == 0)
        def _():
            pl.semaphore_signal(
                barrier, inc=1, device_id={"dp": other, "segment": place + 2}, device_id_type=MESH
            )

        @pl.when(pair == 1)
        def _():
            pl.semaphore_signal(
                barrier, inc=1, device_id={"dp": other, "segment": place - 2}, device_id_type=MESH
            )

    for _, peer in peers:
        pl.semaphore_signal(barrier, inc=1, device_id=peer, device_id_type=MESH)
    gain_acc[0] = jnp.zeros(gain_acc.shape[1:], gain_acc.dtype)
    pl.semaphore_wait(
        barrier,
        len(peers)
        + jnp.where(pair > 0, 1, 0)
        + jnp.where(pair < last, 1, 0)
        + jnp.where(pair <= 1, replicas - 1, 0),
    )

    def send(src, dst, send_sem, recv_sem, peer):
        return pltpu.make_async_remote_copy(
            src_ref=src,
            dst_ref=dst,
            send_sem=send_sem,
            recv_sem=recv_sem,
            device_id=peer,
            device_id_type=MESH,
        )

    def send_forward(i):
        return send(
            y_out.at[i], x_all.at[0, i], fs_sem.at[i], xr_sem.at[0, i], {"segment": place + 2}
        )

    def send_backward(i):
        return send(
            dx_out.at[i], dy_all.at[0, i], bs_sem.at[i], dr_sem.at[0, i], {"segment": place - 2}
        )

    def send_across(off, i):
        return send(
            dx_out.at[i],
            dy_all.at[2 * off, i],
            ac_sem.at[off, i],
            dr_sem.at[2 * off, i],
            {"dp": lax.rem(rep + off, replicas), "segment": place - 2},
        )

    def share(buf, sems, slot, i):
        if slot == 1:
            peer, origin = {"segment": mate}, 0
        elif slot % 2 == 0:
            peer, origin = {"dp": lax.rem(rep + slot // 2, replicas)}, 0
        else:
            peer, origin = {"segment": mate}, slot - 1
        return send(
            buf.at[origin, i], buf.at[slot, i], sems[0].at[slot, i], sems[1].at[slot, i], peer
        )

    xs = (xs_sem, xr_sem)
    ds = (ds_sem, dr_sem)

    def share_own(buf, sems, i):
        for off in range(1, replicas):
            share(buf, sems, 2 * off, i).start()
        share(buf, sems, 1, i).start()

    def hand_on(buf, sems, i):
        for off in range(1, replicas):
            share(buf, sems, 2 * off, i).wait_recv()
            share(buf, sems, 2 * off + 1, i).start()

    def span(i):
        return pl.ds(pl.multiple_of(i * rows, rows), rows)

    def slot_span(s):
        return pl.ds(pl.multiple_of(s * total, total), total)

    def transpose_weights():
        down_t[...] = down[...].T
        up_t[...] = up[...].T

    @pl.when(pair == 0)
    def _():
        for which in (0, 1):
            for m in range(micro):
                feed_copy(which, m).wait()

    load_gain.wait()
    load_up.wait()
    load_down.wait()
    gain_row = gain_ref[0:1, :]

    @pl.when(2 * pair > last)
    def _():
        transpose_weights()

    def forward(i, carry):
        @pl.when(pair > 0)
        def _():
            send_forward(i).wait_recv()

        x = x_all[0, i].astype(jnp.float32)
        xh, inverse = norm_parts(x)
        n = (xh * gain_row).astype(jnp.bfloat16)
        y = x
        for j in range(0, 2 * half, TILE):
            a = jnp.dot(n, up[:, j : j + TILE], preferred_element_type=jnp.float32)
            t = jnp.tanh(GELU_C * (a + CUBIC * a * a * a))
            p = (0.5 * a * (1.0 + t)).astype(jnp.bfloat16)
            a_st[:, j : j + TILE] = a
            t_st[:, j : j + TILE] = t
            p_st[span(i), j : j + TILE] = p
            y = y + jnp.dot(p, down[j : j + TILE, :], preferred_element_type=jnp.float32)
        y = y.astype(jnp.bfloat16)

        @pl.when(pair < last)
        def _():
            y_out[i] = y
            send_forward(i).start()

        @pl.when(pair == last)
        def _():
            dy_all[0, i] = (y.astype(jnp.float32) * loss_scale).astype(jnp.bfloat16)

        xh_st[i] = xh
        inv_st[i] = jnp.broadcast_to(inverse, (rows, 128))
        n_all[span(i), :] = n
        slope_st[i] = gelu_slope(a_st[...], t_st[...])
        return carry

    lax.fori_loop(0, chunks, forward, 0)

    @pl.when(2 * pair <= last)
    def _():
        transpose_weights()

    def share_rows(buf, sems):
        def share_chunk(i, carry):
            share_own(buf, sems, i)
            return carry

        def hand_on_chunk(i, carry):
            hand_on(buf, sems, i)
            return carry

        lax.fori_loop(0, chunks, share_chunk, 0)
        lax.fori_loop(0, chunks, hand_on_chunk, 0)

    def peers_forward():
        share_rows(x_all, xs)
        for s in range(1, slots, 2):
            for i in range(chunks):
                share(x_all, xs, s, i).wait_recv()

        def one(s, carry):
            xh, _ = norm_parts(x_all[s].reshape(total, width).astype(jnp.float32))
            n = (xh * gain_row).astype(jnp.bfloat16)
            n_all[slot_span(s), :] = n
            a = jnp.dot(n, up[:, mine], preferred_element_type=jnp.float32)
            p, slope = gelu_parts(a)
            p_all[slot_span(s), :] = p
            slope_all[slot_span(s), :] = slope
            return carry

        lax.fori_loop(1, slots, one, 0)
        p_all[slot_span(0), :] = p_st[:, mine]

    @pl.when(pair < last - 1)
    def _():
        peers_forward()

    def backward(i, carry):
        @pl.when(pair < last)
        def _():
            send_backward(i).wait_recv()

        @pl.when(pair == 0)
        def _():
            share(dy_all, ds, 1, i).start()

        dy = dy_all[0, i]
        dn = jnp.zeros((rows, width), jnp.float32)
        for j in range(0, 2 * half, TILE):
            dp = jnp.dot(dy, down_t[:, j : j + TILE], preferred_element_type=jnp.float32)
            da = (dp * slope_st[i, :, j : j + TILE]).astype(jnp.bfloat16)
            da_st[span(i), j : j + TILE] = da
            dn = dn + jnp.dot(da, up_t[j : j + TILE, :], preferred_element_type=jnp.float32)
        xh = xh_st[i]
        e = dn * gain_row
        m1 = jnp.mean(e, axis=-1, keepdims=True)
        m2 = jnp.mean(e * xh, axis=-1, keepdims=True)
        inverse = inv_st[i][:, 0:1]
        dx = (dy.astype(jnp.float32) + inverse * (e - m1 - xh * m2)).astype(jnp.bfloat16)

        @pl.when(pair > 0)
        def _():
            dx_out[i] = dx
            send_backward(i).start()

        @pl.when(pair == 1)
        def _():
            for off in range(1, replicas):
                send_across(off, i).start()

        @pl.when((pair == 0) & (i >= LAG))
        def _():
            hand_on(dy_all, ds, i - LAG)

        gain_acc[0] += jnp.sum((dn * xh).reshape(rows // 8, 8, width), axis=0)
        return carry

    lax.fori_loop(0, chunks, backward, 0)
    @pl.when(pair == 0)
    def _():
        for i in range(chunks - LAG, chunks):
            hand_on(dy_all, ds, i)

    @pl.when(pair > 0)
    def _():
        share_rows(dy_all, ds)

    def send_gain(slot, peer):
        return send(gain_acc.at[0], gain_acc.at[slot], gs_sem.at[slot], gr_sem.at[slot], peer)

    for slot, peer in peers:
        send_gain(slot, peer).start()

    @pl.when(pair >= last - 1)
    def _():
        peers_forward()

    da_all[slot_span(0), :] = da_st[:, mine]
    for s in range(2, slots, 2):
        peer_da(s, slot_span, dy_all, down_t, mine, slope_all, da_all)
    for s in range(1, slots, 2):
        for i in range(chunks):
            share(dy_all, ds, s, i).wait_recv()
        peer_da(s, slot_span, dy_all, down_t, mine, slope_all, da_all)

    if slice_d % 128 == 0:
        cols = pl.ds(pl.multiple_of(rep * slice_d, slice_d), slice_d)
        out_up[...] = dot_tn(n_all[:, cols], da_all[...])
        dy_cols = dy_all[:, :, :, cols].reshape(slots * total, slice_d)
        out_down[...] = dot_tn(p_all[...], dy_cols)
    else:
        whole_up = dot_tn(n_all[...], da_all[...])
        whole_down = dot_tn(p_all[...], dy_all[...].reshape(slots * total, width))
        for j in range(replicas):
            acc_up[j] = whole_up[j * slice_d : (j + 1) * slice_d, :]
            acc_down[j] = whole_down[:, j * slice_d : (j + 1) * slice_d]
        out_up[...] = acc_up[rep]
        out_down[...] = acc_down[rep]

    gains = gain_acc[0]
    for slot, peer in peers:
        send_gain(slot, peer).wait()
        gains = gains + gain_acc[slot]
    gains = jnp.sum(gains, axis=0, keepdims=True)
    wide = out_gain.shape[1]
    for c in (0, 1):
        for j in range(replicas):
            start = c * (width // 2) + j * wide

            @pl.when((core == c) & (rep == j))
            def _():
                out_gain[...] = gains[:, start : start + wide]

    def drain(i, carry):
        for slot in range(1, slots):
            share(x_all, xs, slot, i).wait_send()
            if slot % 2:
                share(dy_all, ds, slot, i).wait_send()

        @pl.when(pair > 0)
        def _():
            for off in range(1, replicas):
                share(dy_all, ds, 2 * off, i).wait_send()

        @pl.when(pair == 1)
        def _():
            for off in range(1, replicas):
                send_across(off, i).wait_send()

        @pl.when(pair < last)
        def _():
            send_forward(i).wait_send()

        @pl.when(pair > 0)
        def _():
            send_backward(i).wait_send()

        return carry

    lax.fori_loop(0, chunks, drain, 0)


def hand_over(*refs):
    for k in range(3):
        refs[3 + k][...] = refs[k][...]


def peer_da(s, slot_span, dy_all, down_t, mine, slope_all, da_all):
    slots, chunks, rows, width = dy_all.shape
    dy = dy_all[s].reshape(chunks * rows, width)
    dp = jnp.dot(dy, down_t[:, mine], preferred_element_type=jnp.float32)
    da_all[slot_span(s), :] = (dp * slope_all[slot_span(s), :]).astype(jnp.bfloat16)


def body(feed_rising, feed_falling, up_weight, down_weight, norm_gain):
    segments = lax.axis_size("segment")
    replicas = lax.axis_size("dp")
    micro, rep_rows, width = feed_rising.shape
    local_rows = rep_rows // 2
    hidden = up_weight.shape[2]
    half = hidden // 2
    loss_scale = 1.0 / math.sqrt(2.0 * micro * rep_rows * replicas)
    chunks = 2 * CHUNKS_PER_RELAY
    rows = 2 * micro * local_rows // chunks
    total = chunks * rows
    slots = 2 * replicas
    slice_d = width // replicas
    bf16, f32 = jnp.bfloat16, jnp.float32
    vmem = pl.BlockSpec(memory_space=pltpu.VMEM)
    hbm = pl.BlockSpec(memory_space=pltpu.HBM)
    spare = (8, 128) if slice_d % 128 == 0 else None
    dma = pltpu.SemaphoreType.DMA
    grads = pl.pallas_call(
        functools.partial(kernel, segments, replicas, loss_scale),
        out_shape=(
            jax.ShapeDtypeStruct((slice_d, half), f32),
            jax.ShapeDtypeStruct((half, slice_d), f32),
            jax.ShapeDtypeStruct((1, width // 2 // replicas), f32),
        ),
        in_specs=[hbm, hbm, hbm, hbm, hbm],
        out_specs=(vmem, vmem, vmem),
        scratch_shapes=[
            pltpu.VMEM((width, hidden), bf16),
            pltpu.VMEM((hidden, width), bf16),
            pltpu.VMEM((hidden, width), bf16),
            pltpu.VMEM((width, hidden), bf16),
            pltpu.VMEM((norm_gain.shape[0], width), f32),
            pltpu.VMEM((slots, chunks, rows, width), bf16),
            pltpu.VMEM((slots, chunks, rows, width), bf16),
            pltpu.VMEM((chunks, rows, width), bf16),
            pltpu.VMEM((chunks, rows, width), bf16),
            pltpu.VMEM((chunks, rows, width), f32),
            pltpu.VMEM((chunks, rows, 128), f32),
            pltpu.VMEM((total, hidden), bf16),
            pltpu.VMEM((chunks, rows, hidden), f32),
            pltpu.VMEM((rows, hidden), f32),
            pltpu.VMEM((rows, hidden), f32),
            pltpu.VMEM((total, hidden), bf16),
            pltpu.VMEM((slots * total, width), bf16),
            pltpu.VMEM((slots * total, half), bf16),
            pltpu.VMEM((slots * total, half), f32),
            pltpu.VMEM((slots * total, half), bf16),
            pltpu.VMEM((slots, 8, width), f32),
            pltpu.VMEM(spare or (replicas, slice_d, half), f32),
            pltpu.VMEM(spare or (replicas, half, slice_d), f32),
            dma((3,)),
            dma((2 * micro,)),
            dma((chunks,)),
            dma((chunks,)),
            dma((replicas, chunks)),
            dma((slots, chunks)),
            dma((slots, chunks)),
            dma((slots, chunks)),
            dma((slots, chunks)),
            dma((slots,)),
            dma((slots,)),
        ],
        compiler_params=pltpu.CompilerParams(
            collective_id=0, has_side_effects=True, vmem_limit_bytes=60 * 1024 * 1024
        ),
        cost_estimate=pl.CostEstimate(
            flops=16 * total * width * hidden,
            bytes_accessed=6 * 1024 * 1024,
            transcendentals=3 * total * hidden,
        ),
        name="relay",
    )(feed_rising, feed_falling, up_weight, down_weight, norm_gain)
    return pl.pallas_call(
        hand_over,
        out_shape=tuple(jax.ShapeDtypeStruct(g.shape, g.dtype) for g in grads),
        in_specs=[vmem] * 3,
        out_specs=(vmem,) * 3,
        name="hand_over",
    )(*grads)


def solution(mesh):
    return jax.shard_map(
        body,
        mesh=mesh,
        in_specs=(
            P(None, "dp", None),
            P(None, "dp", None),
            P("segment", None, None),
            P("segment", None, None),
            P("segment", None),
        ),
        out_specs=(P("dp", "segment"), P("segment", "dp"), P("segment", "dp")),
        check_vma=False,
    )
```

```python
import functools
import math

import jax
import jax.numpy as jnp
from jax import lax
from jax.experimental import pallas as pl
from jax.experimental.pallas import tpu as pltpu
from jax.sharding import PartitionSpec as P

GELU_C = 0.7978845608028654
CUBIC = 0.044715
CHUNKS_PER_RELAY = 2
LAG = 3
TILE = 256
MESH = pl.DeviceIdType.MESH


def dot_tn(left, right):
    return lax.dot_general(left, right, (((0,), (0,)), ((), ())), preferred_element_type=jnp.float32)


def gelu_slope(pre_act, tangent):
    return 0.5 * (1.0 + tangent) + 0.5 * pre_act * (1.0 - tangent * tangent) * GELU_C * (
        1.0 + 3.0 * CUBIC * pre_act * pre_act
    )


def gelu_parts(pre_act):
    tangent = jnp.tanh(GELU_C * (pre_act + CUBIC * pre_act * pre_act * pre_act))
    value = 0.5 * pre_act * (1.0 + tangent)
    return value.astype(jnp.bfloat16), gelu_slope(pre_act, tangent)


def norm_parts(x):
    xc = x - jnp.mean(x, axis=-1, keepdims=True)
    inverse = lax.rsqrt(jnp.mean(xc * xc, axis=-1, keepdims=True) + 1e-05)
    return xc * inverse, inverse


def kernel(
    segments,
    replicas,
    loss_scale,
    rising,
    falling,
    up_hbm,
    down_hbm,
    gain_hbm,
    out_up,
    out_down,
    out_gain,
    up,
    down,
    up_t,
    down_t,
    gain_ref,
    x_all,
    dy_all,
    y_out,
    dx_out,
    xh_st,
    inv_st,
    p_st,
    slope_st,
    a_st,
    t_st,
    da_st,
    n_all,
    p_all,
    slope_all,
    da_all,
    gain_acc,
    acc_up,
    acc_down,
    load_sem,
    feed_sem,
    fs_sem,
    bs_sem,
    ac_sem,
    xs_sem,
    xr_sem,
    ds_sem,
    dr_sem,
    gs_sem,
    gr_sem,
):
    place = lax.axis_index("segment")
    rep = lax.axis_index("dp")
    pair = place // 2
    core = place % 2
    last = segments // 2 - 1
    slots, chunks, rows, width = x_all.shape
    total = chunks * rows
    half = up.shape[1] // 2
    micro = rising.shape[0]
    local_rows = rising.shape[1] // 2
    mate = place + 1 - 2 * core
    slice_d = width // replicas
    per_chunk = rows // local_rows
    mine = pl.ds(pl.multiple_of(core * half, half), half)

    def feed_copy(which, m):
        flat = which * micro + m
        return pltpu.make_async_copy(
            (rising, falling)[which].at[
                m, pl.ds(pl.multiple_of(core * local_rows, local_rows), local_rows), :
            ],
            x_all.at[0, flat // per_chunk, pl.ds((flat % per_chunk) * local_rows, local_rows), :],
            feed_sem.at[flat],
        )

    load_gain = pltpu.make_async_copy(gain_hbm, gain_ref, load_sem.at[2])
    load_up = pltpu.make_async_copy(up_hbm.at[0], up, load_sem.at[0])
    load_down = pltpu.make_async_copy(down_hbm.at[0], down, load_sem.at[1])

    @pl.when(pair == 0)
    def _():
        for which in (0, 1):
            for m in range(micro):
                feed_copy(which, m).start()

    load_gain.start()
    load_up.start()
    load_down.start()

    peers = [(1, {"segment": mate})]
    for off in range(1, replicas):
        other = lax.rem(rep + off, replicas)
        peers.append((2 * off, {"dp": other}))
        peers.append((2 * off + 1, {"dp": other, "segment": mate}))

    barrier = pltpu.get_barrier_semaphore()

    @pl.when(pair > 0)
    def _():
        pl.semaphore_signal(barrier, inc=1, device_id={"segment": place - 2}, device_id_type=MESH)

    @pl.when(pair < last)
    def _():
        pl.semaphore_signal(barrier, inc=1, device_id={"segment": place + 2}, device_id_type=MESH)

    for off in range(1, replicas):
        other = lax.rem(rep + off, replicas)

        @pl.when(pair == 0)
        def _():
            pl.semaphore_signal(
                barrier, inc=1, device_id={"dp": other, "segment": place + 2}, device_id_type=MESH
            )

        @pl.when(pair == 1)
        def _():
            pl.semaphore_signal(
                barrier, inc=1, device_id={"dp": other, "segment": place - 2}, device_id_type=MESH
            )

    for _, peer in peers:
        pl.semaphore_signal(barrier, inc=1, device_id=peer, device_id_type=MESH)
    gain_acc[0] = jnp.zeros(gain_acc.shape[1:], gain_acc.dtype)
    pl.semaphore_wait(
        barrier,
        len(peers)
        + jnp.where(pair > 0, 1, 0)
        + jnp.where(pair < last, 1, 0)
        + jnp.where(pair <= 1, replicas - 1, 0),
    )

    def send(src, dst, send_sem, recv_sem, peer):
        return pltpu.make_async_remote_copy(
            src_ref=src,
            dst_ref=dst,
            send_sem=send_sem,
            recv_sem=recv_sem,
            device_id=peer,
            device_id_type=MESH,
        )

    def send_forward(i):
        return send(
            y_out.at[i], x_all.at[0, i], fs_sem.at[i], xr_sem.at[0, i], {"segment": place + 2}
        )

    def send_backward(i):
        return send(
            dx_out.at[i], dy_all.at[0, i], bs_sem.at[i], dr_sem.at[0, i], {"segment": place - 2}
        )

    def send_across(off, i):
        return send(
            dx_out.at[i],
            dy_all.at[2 * off, i],
            ac_sem.at[off, i],
            dr_sem.at[2 * off, i],
            {"dp": lax.rem(rep + off, replicas), "segment": place - 2},
        )

    def share(buf, sems, slot, i):
        if slot == 1:
            peer, origin = {"segment": mate}, 0
        elif slot % 2 == 0:
            peer, origin = {"dp": lax.rem(rep + slot // 2, replicas)}, 0
        else:
            peer, origin = {"segment": mate}, slot - 1
        return send(
            buf.at[origin, i], buf.at[slot, i], sems[0].at[slot, i], sems[1].at[slot, i], peer
        )

    xs = (xs_sem, xr_sem)
    ds = (ds_sem, dr_sem)

    def share_own(buf, sems, i):
        for off in range(1, replicas):
            share(buf, sems, 2 * off, i).start()
        share(buf, sems, 1, i).start()

    def hand_on(buf, sems, i):
        for off in range(1, replicas):
            share(buf, sems, 2 * off, i).wait_recv()
            share(buf, sems, 2 * off + 1, i).start()

    def span(i):
        return pl.ds(pl.multiple_of(i * rows, rows), rows)

    def slot_span(s):
        return pl.ds(pl.multiple_of(s * total, total), total)

    def transpose_weights():
        down_t[...] = down[...].T
        up_t[...] = up[...].T

    @pl.when(pair == 0)
    def _():
        for which in (0, 1):
            for m in range(micro):
                feed_copy(which, m).wait()

    load_gain.wait()
    load_up.wait()
    load_down.wait()
    gain_row = gain_ref[0:1, :]

    @pl.when(2 * pair > last)
    def _():
        transpose_weights()

    def forward(i, carry):
        @pl.when(pair > 0)
        def _():
            send_forward(i).wait_recv()

        x = x_all[0, i].astype(jnp.float32)
        xh, inverse = norm_parts(x)
        n = (xh * gain_row).astype(jnp.bfloat16)
        y = x
        for j in range(0, 2 * half, TILE):
            a = jnp.dot(n, up[:, j : j + TILE], preferred_element_type=jnp.float32)
            t = jnp.tanh(GELU_C * (a + CUBIC * a * a * a))
            p = (0.5 * a * (1.0 + t)).astype(jnp.bfloat16)
            a_st[:, j : j + TILE] = a
            t_st[:, j : j + TILE] = t
            p_st[span(i), j : j + TILE] = p
            y = y + jnp.dot(p, down[j : j + TILE, :], preferred_element_type=jnp.float32)
        y = y.astype(jnp.bfloat16)

        @pl.when(pair < last)
        def _():
            y_out[i] = y
            send_forward(i).start()

        @pl.when(pair == last)
        def _():
            dy_all[0, i] = (y.astype(jnp.float32) * loss_scale).astype(jnp.bfloat16)

        xh_st[i] = xh
        inv_st[i] = jnp.broadcast_to(inverse, (rows, 128))
        n_all[span(i), :] = n
        slope_st[i] = gelu_slope(a_st[...], t_st[...])
        return carry

    lax.fori_loop(0, chunks, forward, 0)

    @pl.when(2 * pair <= last)
    def _():
        transpose_weights()

    def share_rows(buf, sems):
        def share_chunk(i, carry):
            share_own(buf, sems, i)
            return carry

        def hand_on_chunk(i, carry):
            hand_on(buf, sems, i)
            return carry

        lax.fori_loop(0, chunks, share_chunk, 0)
        lax.fori_loop(0, chunks, hand_on_chunk, 0)

    def peers_forward():
        share_rows(x_all, xs)
        for s in range(1, slots, 2):
            for i in range(chunks):
                share(x_all, xs, s, i).wait_recv()

        def one(s, carry):
            xh, _ = norm_parts(x_all[s].reshape(total, width).astype(jnp.float32))
            n = (xh * gain_row).astype(jnp.bfloat16)
            n_all[slot_span(s), :] = n
            a = jnp.dot(n, up[:, mine], preferred_element_type=jnp.float32)
            p, slope = gelu_parts(a)
            p_all[slot_span(s), :] = p
            slope_all[slot_span(s), :] = slope
            return carry

        lax.fori_loop(1, slots, one, 0)
        p_all[slot_span(0), :] = p_st[:, mine]

    @pl.when(pair < last - 1)
    def _():
        peers_forward()

    def backward(i, carry):
        @pl.when(pair < last)
        def _():
            send_backward(i).wait_recv()

        @pl.when(pair == 0)
        def _():
            share(dy_all, ds, 1, i).start()

        dy = dy_all[0, i]
        dn = jnp.zeros((rows, width), jnp.float32)
        for j in range(0, 2 * half, TILE):
            dp = jnp.dot(dy, down_t[:, j : j + TILE], preferred_element_type=jnp.float32)
            da = (dp * slope_st[i, :, j : j + TILE]).astype(jnp.bfloat16)
            da_st[span(i), j : j + TILE] = da
            dn = dn + jnp.dot(da, up_t[j : j + TILE, :], preferred_element_type=jnp.float32)
        xh = xh_st[i]
        e = dn * gain_row
        m1 = jnp.mean(e, axis=-1, keepdims=True)
        m2 = jnp.mean(e * xh, axis=-1, keepdims=True)
        inverse = inv_st[i][:, 0:1]
        dx = (dy.astype(jnp.float32) + inverse * (e - m1 - xh * m2)).astype(jnp.bfloat16)

        @pl.when(pair > 0)
        def _():
            dx_out[i] = dx
            send_backward(i).start()

        @pl.when(pair == 1)
        def _():
            for off in range(1, replicas):
                send_across(off, i).start()

        @pl.when((pair == 0) & (i >= LAG))
        def _():
            hand_on(dy_all, ds, i - LAG)

        gain_acc[0] += jnp.sum((dn * xh).reshape(rows // 8, 8, width), axis=0)
        return carry

    lax.fori_loop(0, chunks, backward, 0)
    @pl.when(pair == 0)
    def _():
        for i in range(chunks - LAG, chunks):
            hand_on(dy_all, ds, i)

    @pl.when(pair > 0)
    def _():
        share_rows(dy_all, ds)

    def send_gain(slot, peer):
        return send(gain_acc.at[0], gain_acc.at[slot], gs_sem.at[slot], gr_sem.at[slot], peer)

    for slot, peer in peers:
        send_gain(slot, peer).start()

    @pl.when(pair >= last - 1)
    def _():
        peers_forward()

    da_all[slot_span(0), :] = da_st[:, mine]
    for s in range(2, slots, 2):
        peer_da(s, slot_span, dy_all, down_t, mine, slope_all, da_all)
    for s in range(1, slots, 2):
        for i in range(chunks):
            share(dy_all, ds, s, i).wait_recv()
        peer_da(s, slot_span, dy_all, down_t, mine, slope_all, da_all)

    if slice_d % 128 == 0:
        cols = pl.ds(pl.multiple_of(rep * slice_d, slice_d), slice_d)
        out_up[...] = dot_tn(n_all[:, cols], da_all[...])
        dy_cols = dy_all[:, :, :, cols].reshape(slots * total, slice_d)
        out_down[...] = dot_tn(p_all[...], dy_cols)
    else:
        whole_up = dot_tn(n_all[...], da_all[...])
        whole_down = dot_tn(p_all[...], dy_all[...].reshape(slots * total, width))
        for j in range(replicas):
            acc_up[j] = whole_up[j * slice_d : (j + 1) * slice_d, :]
            acc_down[j] = whole_down[:, j * slice_d : (j + 1) * slice_d]
        out_up[...] = acc_up[rep]
        out_down[...] = acc_down[rep]

    gains = gain_acc[0]
    for slot, peer in peers:
        send_gain(slot, peer).wait()
        gains = gains + gain_acc[slot]
    gains = jnp.sum(gains, axis=0, keepdims=True)
    wide = out_gain.shape[1]
    for c in (0, 1):
        for j in range(replicas):
            start = c * (width // 2) + j * wide

            @pl.when((core == c) & (rep == j))
            def _():
                out_gain[...] = gains[:, start : start + wide]

    def drain(i, carry):
        for slot in range(1, slots):
            share(x_all, xs, slot, i).wait_send()
            if slot % 2:
                share(dy_all, ds, slot, i).wait_send()

        @pl.when(pair > 0)
        def _():
            for off in range(1, replicas):
                share(dy_all, ds, 2 * off, i).wait_send()

        @pl.when(pair == 1)
        def _():
            for off in range(1, replicas):
                send_across(off, i).wait_send()

        @pl.when(pair < last)
        def _():
            send_forward(i).wait_send()

        @pl.when(pair > 0)
        def _():
            send_backward(i).wait_send()

        return carry

    lax.fori_loop(0, chunks, drain, 0)


def hand_over(*refs):
    for k in range(3):
        refs[3 + k][...] = refs[k][...]


def peer_da(s, slot_span, dy_all, down_t, mine, slope_all, da_all):
    slots, chunks, rows, width = dy_all.shape
    dy = dy_all[s].reshape(chunks * rows, width)
    dp = jnp.dot(dy, down_t[:, mine], preferred_element_type=jnp.float32)
    da_all[slot_span(s), :] = (dp * slope_all[slot_span(s), :]).astype(jnp.bfloat16)


def body(feed_rising, feed_falling, up_weight, down_weight, norm_gain):
    segments = lax.axis_size("segment")
    replicas = lax.axis_size("dp")
    micro, rep_rows, width = feed_rising.shape
    local_rows = rep_rows // 2
    hidden = up_weight.shape[2]
    half = hidden // 2
    loss_scale = 1.0 / math.sqrt(2.0 * micro * rep_rows * replicas)
    chunks = 2 * CHUNKS_PER_RELAY
    rows = 2 * micro * local_rows // chunks
    total = chunks * rows
    slots = 2 * replicas
    slice_d = width // replicas
    bf16, f32 = jnp.bfloat16, jnp.float32
    vmem = pl.BlockSpec(memory_space=pltpu.VMEM)
    hbm = pl.BlockSpec(memory_space=pltpu.HBM)
    spare = (8, 128) if slice_d % 128 == 0 else None
    dma = pltpu.SemaphoreType.DMA
    grads = pl.pallas_call(
        functools.partial(kernel, segments, replicas, loss_scale),
        out_shape=(
            jax.ShapeDtypeStruct((slice_d, half), f32),
            jax.ShapeDtypeStruct((half, slice_d), f32),
            jax.ShapeDtypeStruct((1, width // 2 // replicas), f32),
        ),
        in_specs=[hbm, hbm, hbm, hbm, hbm],
        out_specs=(vmem, vmem, vmem),
        scratch_shapes=[
            pltpu.VMEM((width, hidden), bf16),
            pltpu.VMEM((hidden, width), bf16),
            pltpu.VMEM((hidden, width), bf16),
            pltpu.VMEM((width, hidden), bf16),
            pltpu.VMEM((norm_gain.shape[0], width), f32),
            pltpu.VMEM((slots, chunks, rows, width), bf16),
            pltpu.VMEM((slots, chunks, rows, width), bf16),
            pltpu.VMEM((chunks, rows, width), bf16),
            pltpu.VMEM((chunks, rows, width), bf16),
            pltpu.VMEM((chunks, rows, width), f32),
            pltpu.VMEM((chunks, rows, 128), f32),
            pltpu.VMEM((total, hidden), bf16),
            pltpu.VMEM((chunks, rows, hidden), f32),
            pltpu.VMEM((rows, hidden), f32),
            pltpu.VMEM((rows, hidden), f32),
            pltpu.VMEM((total, hidden), bf16),
            pltpu.VMEM((slots * total, width), bf16),
            pltpu.VMEM((slots * total, half), bf16),
            pltpu.VMEM((slots * total, half), f32),
            pltpu.VMEM((slots * total, half), bf16),
            pltpu.VMEM((slots, 8, width), f32),
            pltpu.VMEM(spare or (replicas, slice_d, half), f32),
            pltpu.VMEM(spare or (replicas, half, slice_d), f32),
            dma((3,)),
            dma((2 * micro,)),
            dma((chunks,)),
            dma((chunks,)),
            dma((replicas, chunks)),
            dma((slots, chunks)),
            dma((slots, chunks)),
            dma((slots, chunks)),
            dma((slots, chunks)),
            dma((slots,)),
            dma((slots,)),
        ],
        compiler_params=pltpu.CompilerParams(
            collective_id=0, has_side_effects=True, vmem_limit_bytes=60 * 1024 * 1024
        ),
        cost_estimate=pl.CostEstimate(
            flops=16 * total * width * hidden,
            bytes_accessed=6 * 1024 * 1024,
            transcendentals=3 * total * hidden,
        ),
        name="relay",
    )(feed_rising, feed_falling, up_weight, down_weight, norm_gain)
    return pl.pallas_call(
        hand_over,
        out_shape=tuple(jax.ShapeDtypeStruct(g.shape, g.dtype) for g in grads),
        in_specs=[vmem] * 3,
        out_specs=(vmem,) * 3,
        name="hand_over",
    )(*grads)


def solution(mesh):
    return jax.shard_map(
        body,
        mesh=mesh,
        in_specs=(
            P(None, "dp", None),
            P(None, "dp", None),
            P("segment", None, None),
            P("segment", None, None),
            P("segment", None),
        ),
        out_specs=(P("dp", "segment"), P("segment", "dp"), P("segment", "dp")),
        check_vma=False,
    )
```

```python
import functools
import math

import jax
import jax.numpy as jnp
from jax import lax
from jax.experimental import pallas as pl
from jax.experimental.pallas import tpu as pltpu
from jax.sharding import PartitionSpec as P

GELU_C = 0.7978845608028654
CUBIC = 0.044715
CHUNKS_PER_RELAY = 4
LAG = 3
TILE = 1024
MESH = pl.DeviceIdType.MESH


def dot_tn(left, right):
    return lax.dot_general(left, right, (((0,), (0,)), ((), ())), preferred_element_type=jnp.float32)


def gelu_slope(pre_act, tangent):
    return 0.5 * (1.0 + tangent) + 0.5 * pre_act * (1.0 - tangent * tangent) * GELU_C * (
        1.0 + 3.0 * CUBIC * pre_act * pre_act
    )


def gelu_parts(pre_act):
    tangent = jnp.tanh(GELU_C * (pre_act + CUBIC * pre_act * pre_act * pre_act))
    value = 0.5 * pre_act * (1.0 + tangent)
    return value.astype(jnp.bfloat16), gelu_slope(pre_act, tangent)


def norm_parts(x):
    xc = x - jnp.mean(x, axis=-1, keepdims=True)
    inverse = lax.rsqrt(jnp.mean(xc * xc, axis=-1, keepdims=True) + 1e-05)
    return xc * inverse, inverse


def kernel(
    segments,
    replicas,
    loss_scale,
    rising,
    falling,
    up_hbm,
    down_hbm,
    gain_hbm,
    out_up,
    out_down,
    out_gain,
    up,
    down,
    up_t,
    down_t,
    gain_ref,
    x_all,
    dy_all,
    y_out,
    dx_out,
    xh_st,
    inv_st,
    p_st,
    slope_st,
    a_st,
    t_st,
    da_st,
    n_all,
    p_all,
    slope_all,
    da_all,
    gain_acc,
    acc_up,
    acc_down,
    load_sem,
    feed_sem,
    fs_sem,
    bs_sem,
    ac_sem,
    xs_sem,
    xr_sem,
    ds_sem,
    dr_sem,
    gs_sem,
    gr_sem,
):
    place = lax.axis_index("segment")
    rep = lax.axis_index("dp")
    pair = place // 2
    core = place % 2
    last = segments // 2 - 1
    slots, chunks, rows, width = x_all.shape
    total = chunks * rows
    half = up.shape[1] // 2
    micro = rising.shape[0]
    local_rows = rising.shape[1] // 2
    mate = place + 1 - 2 * core
    slice_d = width // replicas
    per_chunk = rows // local_rows
    mine = pl.ds(pl.multiple_of(core * half, half), half)

    def feed_copy(which, m):
        flat = which * micro + m
        return pltpu.make_async_copy(
            (rising, falling)[which].at[
                m, pl.ds(pl.multiple_of(core * local_rows, local_rows), local_rows), :
            ],
            x_all.at[0, flat // per_chunk, pl.ds((flat % per_chunk) * local_rows, local_rows), :],
            feed_sem.at[flat],
        )

    load_gain = pltpu.make_async_copy(gain_hbm, gain_ref, load_sem.at[2])
    load_up = pltpu.make_async_copy(up_hbm.at[0], up, load_sem.at[0])
    load_down = pltpu.make_async_copy(down_hbm.at[0], down, load_sem.at[1])

    @pl.when(pair == 0)
    def _():
        for which in (0, 1):
            for m in range(micro):
                feed_copy(which, m).start()

    load_gain.start()
    load_up.start()
    load_down.start()

    peers = [(1, {"segment": mate})]
    for off in range(1, replicas):
        other = lax.rem(rep + off, replicas)
        peers.append((2 * off, {"dp": other}))
        peers.append((2 * off + 1, {"dp": other, "segment": mate}))

    barrier = pltpu.get_barrier_semaphore()

    @pl.when(pair > 0)
    def _():
        pl.semaphore_signal(barrier, inc=1, device_id={"segment": place - 2}, device_id_type=MESH)

    @pl.when(pair < last)
    def _():
        pl.semaphore_signal(barrier, inc=1, device_id={"segment": place + 2}, device_id_type=MESH)

    for off in range(1, replicas):
        other = lax.rem(rep + off, replicas)

        @pl.when(pair == 0)
        def _():
            pl.semaphore_signal(
                barrier, inc=1, device_id={"dp": other, "segment": place + 2}, device_id_type=MESH
            )

        @pl.when(pair == 1)
        def _():
            pl.semaphore_signal(
                barrier, inc=1, device_id={"dp": other, "segment": place - 2}, device_id_type=MESH
            )

    for _, peer in peers:
        pl.semaphore_signal(barrier, inc=1, device_id=peer, device_id_type=MESH)
    gain_acc[0] = jnp.zeros(gain_acc.shape[1:], gain_acc.dtype)
    pl.semaphore_wait(
        barrier,
        len(peers)
        + jnp.where(pair > 0, 1, 0)
        + jnp.where(pair < last, 1, 0)
        + jnp.where(pair <= 1, replicas - 1, 0),
    )

    def send(src, dst, send_sem, recv_sem, peer):
        return pltpu.make_async_remote_copy(
            src_ref=src,
            dst_ref=dst,
            send_sem=send_sem,
            recv_sem=recv_sem,
            device_id=peer,
            device_id_type=MESH,
        )

    def send_forward(i):
        return send(
            y_out.at[i], x_all.at[0, i], fs_sem.at[i], xr_sem.at[0, i], {"segment": place + 2}
        )

    def send_backward(i):
        return send(
            dx_out.at[i], dy_all.at[0, i], bs_sem.at[i], dr_sem.at[0, i], {"segment": place - 2}
        )

    def send_across(off, i):
        return send(
            dx_out.at[i],
            dy_all.at[2 * off, i],
            ac_sem.at[off, i],
            dr_sem.at[2 * off, i],
            {"dp": lax.rem(rep + off, replicas), "segment": place - 2},
        )

    def share(buf, sems, slot, i):
        if slot == 1:
            peer, origin = {"segment": mate}, 0
        elif slot % 2 == 0:
            peer, origin = {"dp": lax.rem(rep + slot // 2, replicas)}, 0
        else:
            peer, origin = {"segment": mate}, slot - 1
        return send(
            buf.at[origin, i], buf.at[slot, i], sems[0].at[slot, i], sems[1].at[slot, i], peer
        )

    xs = (xs_sem, xr_sem)
    ds = (ds_sem, dr_sem)

    def share_own(buf, sems, i):
        for off in range(1, replicas):
            share(buf, sems, 2 * off, i).start()
        share(buf, sems, 1, i).start()

    def hand_on(buf, sems, i):
        for off in range(1, replicas):
            share(buf, sems, 2 * off, i).wait_recv()
            share(buf, sems, 2 * off + 1, i).start()

    def span(i):
        return pl.ds(pl.multiple_of(i * rows, rows), rows)

    def slot_span(s):
        return pl.ds(pl.multiple_of(s * total, total), total)

    def transpose_weights():
        down_t[...] = down[...].T
        up_t[...] = up[...].T

    @pl.when(pair == 0)
    def _():
        for which in (0, 1):
            for m in range(micro):
                feed_copy(which, m).wait()

    load_gain.wait()
    load_up.wait()
    load_down.wait()
    gain_row = gain_ref[0:1, :]

    @pl.when(2 * pair > last)
    def _():
        transpose_weights()

    def forward(i, carry):
        @pl.when(pair > 0)
        def _():
            send_forward(i).wait_recv()

        x = x_all[0, i].astype(jnp.float32)
        xh, inverse = norm_parts(x)
        n = (xh * gain_row).astype(jnp.bfloat16)
        y = x
        for j in range(0, 2 * half, TILE):
            a = jnp.dot(n, up[:, j : j + TILE], preferred_element_type=jnp.float32)
            t = jnp.tanh(GELU_C * (a + CUBIC * a * a * a))
            p = (0.5 * a * (1.0 + t)).astype(jnp.bfloat16)
            a_st[:, j : j + TILE] = a
            t_st[:, j : j + TILE] = t
            p_st[span(i), j : j + TILE] = p
            y = y + jnp.dot(p, down[j : j + TILE, :], preferred_element_type=jnp.float32)
        y = y.astype(jnp.bfloat16)

        @pl.when(pair < last)
        def _():
            y_out[i] = y
            send_forward(i).start()

        @pl.when(pair == last)
        def _():
            dy_all[0, i] = (y.astype(jnp.float32) * loss_scale).astype(jnp.bfloat16)

        xh_st[i] = xh
        inv_st[i] = jnp.broadcast_to(inverse, (rows, 128))
        n_all[span(i), :] = n
        slope_st[i] = gelu_slope(a_st[...], t_st[...])
        return carry

    lax.fori_loop(0, chunks, forward, 0)

    @pl.when(2 * pair <= last)
    def _():
        transpose_weights()

    def share_rows(buf, sems):
        def share_chunk(i, carry):
            share_own(buf, sems, i)
            return carry

        def hand_on_chunk(i, carry):
            hand_on(buf, sems, i)
            return carry

        lax.fori_loop(0, chunks, share_chunk, 0)
        lax.fori_loop(0, chunks, hand_on_chunk, 0)

    def peers_forward():
        share_rows(x_all, xs)
        for s in range(1, slots, 2):
            for i in range(chunks):
                share(x_all, xs, s, i).wait_recv()

        def one(s, carry):
            xh, _ = norm_parts(x_all[s].reshape(total, width).astype(jnp.float32))
            n = (xh * gain_row).astype(jnp.bfloat16)
            n_all[slot_span(s), :] = n
            a = jnp.dot(n, up[:, mine], preferred_element_type=jnp.float32)
            p, slope = gelu_parts(a)
            p_all[slot_span(s), :] = p
            slope_all[slot_span(s), :] = slope
            return carry

        lax.fori_loop(1, slots, one, 0)
        p_all[slot_span(0), :] = p_st[:, mine]

    @pl.when(pair < last - 1)
    def _():
        peers_forward()

    def backward(i, carry):
        @pl.when(pair < last)
        def _():
            send_backward(i).wait_recv()

        @pl.when(pair == 0)
        def _():
            share(dy_all, ds, 1, i).start()

        dy = dy_all[0, i]
        dn = jnp.zeros((rows, width), jnp.float32)
        for j in range(0, 2 * half, TILE):
            dp = jnp.dot(dy, down_t[:, j : j + TILE], preferred_element_type=jnp.float32)
            da = (dp * slope_st[i, :, j : j + TILE]).astype(jnp.bfloat16)
            da_st[span(i), j : j + TILE] = da
            dn = dn + jnp.dot(da, up_t[j : j + TILE, :], preferred_element_type=jnp.float32)
        xh = xh_st[i]
        e = dn * gain_row
        m1 = jnp.mean(e, axis=-1, keepdims=True)
        m2 = jnp.mean(e * xh, axis=-1, keepdims=True)
        inverse = inv_st[i][:, 0:1]
        dx = (dy.astype(jnp.float32) + inverse * (e - m1 - xh * m2)).astype(jnp.bfloat16)

        @pl.when(pair > 0)
        def _():
            dx_out[i] = dx
            send_backward(i).start()

        @pl.when(pair == 1)
        def _():
            for off in range(1, replicas):
                send_across(off, i).start()

        @pl.when((pair == 0) & (i >= LAG))
        def _():
            hand_on(dy_all, ds, i - LAG)

        gain_acc[0] += jnp.sum((dn * xh).reshape(rows // 8, 8, width), axis=0)
        return carry

    lax.fori_loop(0, chunks, backward, 0)
    @pl.when(pair == 0)
    def _():
        for i in range(chunks - LAG, chunks):
            hand_on(dy_all, ds, i)

    @pl.when(pair > 0)
    def _():
        share_rows(dy_all, ds)

    def send_gain(slot, peer):
        return send(gain_acc.at[0], gain_acc.at[slot], gs_sem.at[slot], gr_sem.at[slot], peer)

    for slot, peer in peers:
        send_gain(slot, peer).start()

    @pl.when(pair >= last - 1)
    def _():
        peers_forward()

    da_all[slot_span(0), :] = da_st[:, mine]
    for s in range(2, slots, 2):
        peer_da(s, slot_span, dy_all, down_t, mine, slope_all, da_all)
    for s in range(1, slots, 2):
        for i in range(chunks):
            share(dy_all, ds, s, i).wait_recv()
        peer_da(s, slot_span, dy_all, down_t, mine, slope_all, da_all)

    if slice_d % 128 == 0:
        cols = pl.ds(pl.multiple_of(rep * slice_d, slice_d), slice_d)
        out_up[...] = dot_tn(n_all[:, cols], da_all[...])
        dy_cols = dy_all[:, :, :, cols].reshape(slots * total, slice_d)
        out_down[...] = dot_tn(p_all[...], dy_cols)
    else:
        whole_up = dot_tn(n_all[...], da_all[...])
        whole_down = dot_tn(p_all[...], dy_all[...].reshape(slots * total, width))
        for j in range(replicas):
            acc_up[j] = whole_up[j * slice_d : (j + 1) * slice_d, :]
            acc_down[j] = whole_down[:, j * slice_d : (j + 1) * slice_d]
        out_up[...] = acc_up[rep]
        out_down[...] = acc_down[rep]

    gains = gain_acc[0]
    for slot, peer in peers:
        send_gain(slot, peer).wait()
        gains = gains + gain_acc[slot]
    gains = jnp.sum(gains, axis=0, keepdims=True)
    wide = out_gain.shape[1]
    for c in (0, 1):
        for j in range(replicas):
            start = c * (width // 2) + j * wide

            @pl.when((core == c) & (rep == j))
            def _():
                out_gain[...] = gains[:, start : start + wide]

    def drain(i, carry):
        for slot in range(1, slots):
            share(x_all, xs, slot, i).wait_send()
            if slot % 2:
                share(dy_all, ds, slot, i).wait_send()

        @pl.when(pair > 0)
        def _():
            for off in range(1, replicas):
                share(dy_all, ds, 2 * off, i).wait_send()

        @pl.when(pair == 1)
        def _():
            for off in range(1, replicas):
                send_across(off, i).wait_send()

        @pl.when(pair < last)
        def _():
            send_forward(i).wait_send()

        @pl.when(pair > 0)
        def _():
            send_backward(i).wait_send()

        return carry

    lax.fori_loop(0, chunks, drain, 0)


def hand_over(*refs):
    for k in range(3):
        refs[3 + k][...] = refs[k][...]


def peer_da(s, slot_span, dy_all, down_t, mine, slope_all, da_all):
    slots, chunks, rows, width = dy_all.shape
    dy = dy_all[s].reshape(chunks * rows, width)
    dp = jnp.dot(dy, down_t[:, mine], preferred_element_type=jnp.float32)
    da_all[slot_span(s), :] = (dp * slope_all[slot_span(s), :]).astype(jnp.bfloat16)


def body(feed_rising, feed_falling, up_weight, down_weight, norm_gain):
    segments = lax.axis_size("segment")
    replicas = lax.axis_size("dp")
    micro, rep_rows, width = feed_rising.shape
    local_rows = rep_rows // 2
    hidden = up_weight.shape[2]
    half = hidden // 2
    loss_scale = 1.0 / math.sqrt(2.0 * micro * rep_rows * replicas)
    chunks = 2 * CHUNKS_PER_RELAY
    rows = 2 * micro * local_rows // chunks
    total = chunks * rows
    slots = 2 * replicas
    slice_d = width // replicas
    bf16, f32 = jnp.bfloat16, jnp.float32
    vmem = pl.BlockSpec(memory_space=pltpu.VMEM)
    hbm = pl.BlockSpec(memory_space=pltpu.HBM)
    spare = (8, 128) if slice_d % 128 == 0 else None
    dma = pltpu.SemaphoreType.DMA
    grads = pl.pallas_call(
        functools.partial(kernel, segments, replicas, loss_scale),
        out_shape=(
            jax.ShapeDtypeStruct((slice_d, half), f32),
            jax.ShapeDtypeStruct((half, slice_d), f32),
            jax.ShapeDtypeStruct((1, width // 2 // replicas), f32),
        ),
        in_specs=[hbm, hbm, hbm, hbm, hbm],
        out_specs=(vmem, vmem, vmem),
        scratch_shapes=[
            pltpu.VMEM((width, hidden), bf16),
            pltpu.VMEM((hidden, width), bf16),
            pltpu.VMEM((hidden, width), bf16),
            pltpu.VMEM((width, hidden), bf16),
            pltpu.VMEM((norm_gain.shape[0], width), f32),
            pltpu.VMEM((slots, chunks, rows, width), bf16),
            pltpu.VMEM((slots, chunks, rows, width), bf16),
            pltpu.VMEM((chunks, rows, width), bf16),
            pltpu.VMEM((chunks, rows, width), bf16),
            pltpu.VMEM((chunks, rows, width), f32),
            pltpu.VMEM((chunks, rows, 128), f32),
            pltpu.VMEM((total, hidden), bf16),
            pltpu.VMEM((chunks, rows, hidden), f32),
            pltpu.VMEM((rows, hidden), f32),
            pltpu.VMEM((rows, hidden), f32),
            pltpu.VMEM((total, hidden), bf16),
            pltpu.VMEM((slots * total, width), bf16),
            pltpu.VMEM((slots * total, half), bf16),
            pltpu.VMEM((slots * total, half), f32),
            pltpu.VMEM((slots * total, half), bf16),
            pltpu.VMEM((slots, 8, width), f32),
            pltpu.VMEM(spare or (replicas, slice_d, half), f32),
            pltpu.VMEM(spare or (replicas, half, slice_d), f32),
            dma((3,)),
            dma((2 * micro,)),
            dma((chunks,)),
            dma((chunks,)),
            dma((replicas, chunks)),
            dma((slots, chunks)),
            dma((slots, chunks)),
            dma((slots, chunks)),
            dma((slots, chunks)),
            dma((slots,)),
            dma((slots,)),
        ],
        compiler_params=pltpu.CompilerParams(
            collective_id=0, has_side_effects=True, vmem_limit_bytes=60 * 1024 * 1024
        ),
        cost_estimate=pl.CostEstimate(
            flops=16 * total * width * hidden,
            bytes_accessed=6 * 1024 * 1024,
            transcendentals=3 * total * hidden,
        ),
        name="relay",
    )(feed_rising, feed_falling, up_weight, down_weight, norm_gain)
    return pl.pallas_call(
        hand_over,
        out_shape=tuple(jax.ShapeDtypeStruct(g.shape, g.dtype) for g in grads),
        in_specs=[vmem] * 3,
        out_specs=(vmem,) * 3,
        name="hand_over",
    )(*grads)


def solution(mesh):
    return jax.shard_map(
        body,
        mesh=mesh,
        in_specs=(
            P(None, "dp", None),
            P(None, "dp", None),
            P("segment", None, None),
            P("segment", None, None),
            P("segment", None),
        ),
        out_specs=(P("dp", "segment"), P("segment", "dp"), P("segment", "dp")),
        check_vma=False,
    )
```
